32 devices in a mesh: slab: 4 (over y, x), coil: 8 (over z, core).
Axes of the slice: x: 2, y: 2, z: 4, core: 2. Of those that a mesh axis runs over, the one named last changes fastest.
Arguments:
- kspace: bfloat16 [4, 8, 2, 512, 512], P('slab', 'coil'), may hold values from -6 to 6
- sensitivity: bfloat16 [4, 8, 2, 512, 512], P('slab', 'coil'), may hold values from -2 to 2
- sampling: int32 [4, 512, 512], P('slab'), may hold values 0 or 1
Outputs:
- estimate: float32 [4, 2, 512, 512], P('slab', None, 'coil')
The draws below stay inside these ranges and needn't reach their ends.
All inputs are finite; a program needn't handle non-finite values. No bound on the sum of `sampling` on one device may be relied on, other than what follows from the above.
Results may differ from the reference program's by a relative error of at most 0.005.
Values sent between devices are 32-bit elements; how exact they have to be, the bound alone decides.
No kernel may reach another device: no remote copies, remote signals or barrier semaphores. Data moves between devices by JAX's collectives and lax.ppermute only.
A program may use at most 128 MiB of HBM per device.

```python
import math
from functools import partial
import jax
import jax.numpy as jnp
from jax import lax

NY = 512
NZ = 512
ITERS = 1
COILS = 8
SLICES = 4


def plant(values, rng, low, largest):
    dims = values.shape
    spot = [jax.random.randint(jax.random.fold_in(rng, axis), (), 0, dims[axis]) for axis in range(len(dims))]
    values = values.at[tuple(spot)].set(low)
    longest = dims.index(max(dims))
    spot[longest] = (spot[longest] + 1) % dims[longest]
    return values.at[tuple(spot)].set(largest)


def shard_levels(rng, shape, cuts, least, largest):
    level, own = 1.0, jax.random.fold_in(rng, 6)
    for dim, shards_of in cuts:
        draws = jnp.exp(jax.random.uniform(jax.random.fold_in(own, dim), (shards_of,), jnp.float32, least / len(cuts), largest / len(cuts)))
        level = level * jnp.repeat(draws, shape[dim] // shards_of).reshape([-1 if axis == dim else 1 for axis in range(len(shape))])
    return level


def centred(key, shape, deviation, most, split=(), kind=jnp.bfloat16):
    drawn = deviation * jax.random.normal(key, shape, jnp.float32)
    if split:
        drawn = drawn * shard_levels(key, shape, split, -0.22, 0.18)
    return jnp.clip(drawn, -most, most).astype(kind)


def setup_inputs(seed: int = 0) -> dict:
    key_list = jax.random.split(jax.random.key(seed), 4)
    return {
        "kspace": centred(key_list[0], (SLICES, COILS, 2, NY, NZ), 1.0, 6.0, ((0, 4), (1, 8))),
        "sensitivity": centred(key_list[1], (SLICES, COILS, 2, NY, NZ), COILS ** -0.5, 2.0, ((0, 4), (1, 8))),
        "sampling": plant((jax.random.randint(key_list[2], (SLICES, NY, NZ), 0, 3) < 1).astype(jnp.int32), jax.random.fold_in(key_list[2], 1), 0, 1),
    }


STEP_SIZE = 0.25
TV_WEIGHT = 0.5
TV_SMOOTH = 0.25

def dft_tables(length):
    indices = jnp.arange(length, dtype=jnp.int32)
    products = indices[:, None] * indices[None, :] % length
    angles = products.astype(jnp.float32) * (2.0 * math.pi / length)
    factor = 1.0 / math.sqrt(length)
    return ((jnp.cos(angles) * factor).astype(jnp.bfloat16), (-jnp.sin(angles) * factor).astype(jnp.bfloat16))

def right_table(length, sign):
    cosine, sine = dft_tables(length)
    signed = sine if sign > 0 else -sine
    return jnp.stack([jnp.stack([cosine, signed], axis=1), jnp.stack([-signed, cosine], axis=1)], axis=0)

def left_table(length, sign):
    cosine, sine = dft_tables(length)
    signed = sine if sign > 0 else -sine
    return jnp.stack([jnp.stack([cosine, -signed], axis=1), jnp.stack([signed, cosine], axis=1)], axis=0)

def all_tables(rows, cols):
    return (left_table(rows, 1), left_table(rows, -1), right_table(cols, 1), right_table(cols, -1))

def apply_right(pair, table):
    return jnp.einsum('pyz,pzqw->qyw', pair.astype(jnp.float32), table.astype(jnp.float32))

def apply_left(table, pair):
    return jnp.einsum('qypk,pkz->qyz', table.astype(jnp.float32), pair.astype(jnp.float32))

def coil_adjoint(tables, resid, sens_pair):
    row_fwd, row_adj, col_fwd, col_adj = tables
    upper = apply_left(row_adj, resid).astype(jnp.bfloat16)
    back = apply_right(upper, col_adj)
    sens_real = sens_pair[0].astype(jnp.float32)
    sens_imag = sens_pair[1].astype(jnp.float32)
    return jnp.stack([sens_real * back[0] + sens_imag * back[1], sens_real * back[1] - sens_imag * back[0]])

def coil_zero_filled(tables, inputs):
    sens_pair, kspace_pair, sampling_slice = inputs
    measured = kspace_pair * sampling_slice.astype(jnp.bfloat16)[None]
    return coil_adjoint(tables, measured, sens_pair)

def coil_gradient(tables, inputs):
    sens_pair, kspace_pair, sampling_slice, estimate_pair = inputs
    row_fwd, row_adj, col_fwd, col_adj = tables
    sens_real = sens_pair[0].astype(jnp.float32)
    sens_imag = sens_pair[1].astype(jnp.float32)
    coil_pair = jnp.stack([sens_real * estimate_pair[0] - sens_imag * estimate_pair[1], sens_real * estimate_pair[1] + sens_imag * estimate_pair[0]]).astype(jnp.bfloat16)
    middle = apply_right(coil_pair, col_fwd).astype(jnp.bfloat16)
    freq = apply_left(row_fwd, middle)
    weight = sampling_slice.astype(jnp.float32)[None]
    resid = (weight * (freq - kspace_pair.astype(jnp.float32))).astype(jnp.bfloat16)
    return coil_adjoint(tables, resid, sens_pair)

def coil_sum(per_coil, sensitivity, kspace, sampling, extras):
    mapped = (sensitivity, kspace, sampling) + extras
    vmap_axes = (0, 0, None) + (None,) * len(extras)

    def one_slice(inputs):
        coil_terms = jax.vmap(per_coil, in_axes=(vmap_axes,))(inputs)
        return lax.optimization_barrier(jnp.sum(coil_terms, axis=0))
    return lax.map(one_slice, mapped)

def tv_gradient(volume, padded):
    differences = [jnp.roll(volume, -1, axis=axis_id) - volume for axis_id in (0, 2, 3)]
    squares = differences[0] * differences[0] + differences[1] * differences[1] + differences[2] * differences[2]
    weights = lax.rsqrt(lax.optimization_barrier(jnp.sum(squares, axis=1, keepdims=True)) + TV_SMOOTH)
    result = jnp.zeros_like(volume)
    for axis_id, change in zip((0, 2, 3), differences):
        flux_term = weights * change
        result = result + (jnp.roll(flux_term, 1, axis=axis_id) - flux_term)
    for axis_id in padded:
        result = lax.slice_in_dim(result, 1, result.shape[axis_id] - 1, axis=axis_id)
    return result

def reference(kspace, sensitivity, sampling):
    tables = all_tables(sampling.shape[1], sampling.shape[2])
    estimate = coil_sum(partial(coil_zero_filled, tables), sensitivity, kspace, sampling, ())
    for iteration in range(ITERS):
        gradient = coil_sum(partial(coil_gradient, tables), sensitivity, kspace, sampling, (estimate,))
        estimate = estimate - STEP_SIZE * (gradient + TV_WEIGHT * tv_gradient(estimate, ()))
    return estimate
```

```python
from functools import partial
import math

import jax
import jax.numpy as jnp
import ml_dtypes
import numpy as np
from jax import lax
from jax.experimental import pallas as pl
from jax.experimental.pallas import tpu as pltpu
from jax.sharding import PartitionSpec as P

STEP_SIZE = 0.25
TV_WEIGHT = 0.5
TV_SMOOTH = 0.25

F32 = jnp.float32
BF16 = jnp.bfloat16
VMEM = pl.BlockSpec(memory_space=pltpu.VMEM)
SMEM = pl.BlockSpec(memory_space=pltpu.SMEM)
PARAMS = pltpu.CompilerParams(vmem_limit_bytes=24 * 2**20)


def dft_table(length):
    indices = np.arange(length, dtype=np.int64)
    angles = (indices[:, None] * indices[None, :] % length) * (2.0 * math.pi / length)
    factor = 1.0 / math.sqrt(length)
    cosine = np.cos(angles) * factor
    sine = -np.sin(angles) * factor
    return np.block([[cosine, sine], [-sine, cosine]]).astype(ml_dtypes.bfloat16)


def swap(value, bit):
    count = lax.axis_size("coil")
    return lax.ppermute(value, "coil", [(i, i ^ (1 << bit)) for i in range(count)])


def halving_order(bits):
    masks = [0]
    for bit in reversed(bits):
        masks = masks + [mask | (1 << bit) for mask in masks]
    return masks


def flops(cost):
    return pl.CostEstimate(flops=cost, bytes_accessed=4 * 2**20, transcendentals=0)


def mask_kernel(kspace, sampling, out):
    weight = sampling[...].astype(F32).astype(BF16)
    out[0] = kspace[0] * weight
    out[1] = kspace[1] * weight


def adjoint_kernel(groups, size, me, table, data, sens, *refs):
    outs, (lhs, rhs) = refs[: len(groups)], refs[len(groups) :]
    length = sens.shape[1]
    device = me[0]
    starts = [pl.multiple_of(start(device), size) for group in groups for start in group]
    total = len(starts) * size
    for block, start in enumerate(starts):
        at = block * size
        lhs[at : at + size, :] = table[pl.ds(start, size), :]
        lhs[total + at : total + at + size, :] = table[pl.ds(length + start, size), :]
    upper = jnp.dot(lhs[...], data[...], preferred_element_type=F32).astype(BF16)
    real, imag = upper[:total], upper[total:]
    rhs[:total, :length] = imag
    rhs[:total, length:] = real
    rhs[total:, :length] = -real
    rhs[total:, length:] = imag
    back = jnp.dot(rhs[...], table[:, length:], preferred_element_type=F32)
    block = 0
    for group, out in zip(groups, outs):
        for place in range(len(group)):
            at, rows = block * size, pl.ds(starts[block], size)
            real, imag = back[at : at + size], back[total + at : total + at + size]
            sens_real, sens_imag = sens[0, rows, :].astype(F32), sens[1, rows, :].astype(F32)
            out[place, 0] = sens_real * real + sens_imag * imag
            out[place, 1] = sens_real * imag - sens_imag * real
            block += 1


def adjoint(groups, size, me, table, data, sens):
    length = sens.shape[1]
    total = size * sum(len(group) for group in groups)
    return pl.pallas_call(
        partial(adjoint_kernel, groups, size),
        out_shape=[jax.ShapeDtypeStruct((len(group), 2, size, length), F32) for group in groups],
        in_specs=[SMEM, VMEM, VMEM, VMEM],
        out_specs=[VMEM] * len(groups),
        scratch_shapes=[pltpu.VMEM((2 * total, 2 * length), BF16)] * 2,
        compiler_params=PARAMS,
        cost_estimate=flops(16 * total * length * length),
        name="adjoint",
    )(me, table, data.reshape(2 * length, length), sens)


def forward_kernel(chunk, masks, last, me, table, sens, *refs):
    pieces, refs = refs[: len(masks)], refs[len(masks) :]
    if last:
        before, kspace, sampling, volume, out, lhs, mid, neg = refs
    else:
        volume, out, lhs, mid, neg = refs
    length = sens.shape[1]
    size = pieces[0].shape[1]
    rows = size * len(masks)
    low = me[0] & (len(masks) - 1)
    for mask, piece in zip(masks, pieces):
        start = pl.multiple_of((low ^ mask) * size, size)
        real, imag = piece[0], piece[1]
        volume[0, pl.ds(start, size), :] = real
        volume[1, pl.ds(start, size), :] = imag
        at = pl.ds(pl.multiple_of(chunk * rows + start, size), size)
        sens_real, sens_imag = sens[0, at, :].astype(F32), sens[1, at, :].astype(F32)
        coil_real = (sens_real * real - sens_imag * imag).astype(BF16)
        coil_imag = (sens_real * imag + sens_imag * real).astype(BF16)
        top, bottom = pl.ds(start, size), pl.ds(pl.multiple_of(rows + start, size), size)
        lhs[top, :length] = -coil_imag
        lhs[top, length:] = coil_real
        lhs[bottom, :length] = coil_real
        lhs[bottom, length:] = coil_imag
    middle = jnp.dot(lhs[...], table[:, length:], preferred_element_type=F32).astype(BF16)
    mid[:, :length] = middle[:rows]
    mid[:, length:] = middle[rows:]
    neg[:, :length] = -middle[rows:]
    neg[:, length:] = middle[:rows]
    first = chunk * rows
    cosine = table[:length, first : first + rows]
    sine = table[:length, length + first : length + first + rows]
    freq = jnp.dot(cosine, mid[...], preferred_element_type=F32)
    freq += jnp.dot(sine, neg[...], preferred_element_type=F32)
    if last:
        freq += before[...]
        weight = sampling[...].astype(F32)
        out[0] = (weight * (freq[:, :length] - kspace[0].astype(F32))).astype(BF16)
        out[1] = (weight * (freq[:, length:] - kspace[1].astype(F32))).astype(BF16)
    else:
        out[...] = freq


def forward(chunk, masks, me, table, sens, pieces, rest):
    length = sens.shape[1]
    rows = pieces[0].shape[1] * len(masks)
    last = bool(rest)
    freq = jax.ShapeDtypeStruct((length, 2 * length), F32)
    resid = jax.ShapeDtypeStruct((2, length, length), BF16)
    return pl.pallas_call(
        partial(forward_kernel, chunk, masks, last),
        out_shape=[jax.ShapeDtypeStruct((2, rows, length), F32), resid if last else freq],
        in_specs=[SMEM] + [VMEM] * (2 + len(pieces) + len(rest)),
        out_specs=[VMEM] * 2,
        scratch_shapes=[pltpu.VMEM((2 * rows, 2 * length), BF16)]
        + [pltpu.VMEM((rows, 2 * length), BF16)] * 2,
        compiler_params=PARAMS,
        cost_estimate=flops(16 * rows * length * length),
        name="forward",
    )(me, table, sens, *pieces, *rest)


def extend_kernel(size, me, low, high, out):
    half = low.shape[1]
    start = me[0] * size
    for at, first, count in ((0, start - 8, 8), (8, start, size), (8 + size, start + size, 8)):
        first = (first + 2 * half) & (2 * half - 1)

        @pl.when(first < half)
        def _():
            out[:, at : at + count, :] = low[:, pl.ds(pl.multiple_of(first, 8), count), :]

        @pl.when(first >= half)
        def _():
            out[:, at : at + count, :] = high[:, pl.ds(pl.multiple_of(first - half, 8), count), :]


def tv_kernel(own, before, after, out):
    size = out.shape[1]
    length = out.shape[2]

    def parts(ref, first, count):
        return [ref[part, first : first + count, :] for part in (0, 1)]

    def next_column(values):
        return [pltpu.roll(value, length - 1, 1) for value in values]

    def minus(left, right):
        return [a - b for a, b in zip(left, right)]

    def fluxes(here, slices, rows):
        columns = minus(next_column(here), here)
        squares = TV_SMOOTH
        for change in (slices, rows, columns):
            squares = squares + (change[0] * change[0] + change[1] * change[1])
        weight = lax.rsqrt(squares)
        return [[weight * value for value in change] for change in (slices, rows, columns)]

    count = size + 1
    here = parts(own, 7, count)
    slices, rows, columns = fluxes(
        here, minus(parts(after, 7, count), here), minus(parts(own, 8, count), here)
    )
    back = parts(before, 8, size)
    center = parts(own, 8, size)
    back_slices, _, _ = fluxes(back, minus(center, back), minus(parts(before, 9, size), back))
    for part in (0, 1):
        col = columns[part][1:]
        tv = (
            (back_slices[part] - slices[part][1:])
            + (rows[part][:-1] - rows[part][1:])
            + (pltpu.roll(col, 1, 1) - col)
        )
        out[part] = center[part] - (STEP_SIZE * TV_WEIGHT) * tv


def shards(kspace, sensitivity, sampling):
    kspace, sens, sampling = kspace[0, 0], sensitivity[0, 0], sampling[0]
    length = sampling.shape[0]
    count = lax.axis_size("coil")
    slabs = lax.axis_size("slab")
    top = count.bit_length() - 2
    size = length // count
    half = count // 2
    table = jnp.asarray(dft_table(length))
    me = lax.axis_index("coil").astype(jnp.int32).reshape(1)

    measured = pl.pallas_call(
        mask_kernel,
        out_shape=jax.ShapeDtypeStruct(kspace.shape, BF16),
        in_specs=[VMEM, VMEM],
        out_specs=VMEM,
        compiler_params=PARAMS,
        name="measured",
    )(kspace, sampling)

    def chunk_start(chunk, mask):
        return lambda device: (chunk * half + ((device & (half - 1)) ^ mask)) * size

    order = halving_order(range(1, top))
    groups = []
    for chunk in (0, 1):
        groups.append([chunk_start(chunk, mask | 1) for mask in order])
        groups.append([chunk_start(chunk, mask) for mask in order])
    others, owns = [None, None], [None, None]
    (others[0],) = adjoint(groups[0:1], size, me, table, measured, sens)
    (owns[0],) = adjoint(groups[1:2], size, me, table, measured, sens)
    others[1], owns[1] = adjoint(groups[2:4], size, me, table, measured, sens)

    masks = list(range(half))
    freq, volumes = None, []
    for chunk in (0, 1):
        current = owns[chunk] + swap(others[chunk], 0)
        for bit in range(1, top):
            middle = current.shape[0] // 2
            current = current[:middle] + swap(current[middle:], bit)
        current = current[0]
        pieces = {0: current + swap(current, top)}
        for bit in reversed(range(top)):
            for mask in list(pieces):
                pieces[mask | (1 << bit)] = swap(pieces[mask], bit)
        rest = () if chunk == 0 else (freq, kspace, sampling)
        volume, freq = forward(
            chunk, masks, me, table, sens, [pieces[mask] for mask in masks], rest
        )
        volumes.append(volume)
    resid = freq

    parts = 2 if size >= 32 else 1
    part_size = size // parts

    def row_start(part, mask):
        return lambda device: (device ^ mask) * size + part * part_size

    order = halving_order(range(1, top + 1))
    gradient = []
    for part in range(parts):
        group = [row_start(part, mask | 1) for mask in order]
        (other,) = adjoint([group], part_size, me, table, resid, sens)
        group = [row_start(part, mask) for mask in order]
        (own,) = adjoint([group], part_size, me, table, resid, sens)
        current = own + swap(other, 0)
        for bit in range(1, top + 1):
            middle = current.shape[0] // 2
            current = current[:middle] + swap(current[middle:], bit)
        gradient.append(current[0])

    extended = pl.pallas_call(
        partial(extend_kernel, size),
        out_shape=jax.ShapeDtypeStruct((2, size + 16, length), F32),
        in_specs=[SMEM, VMEM, VMEM],
        out_specs=VMEM,
        compiler_params=PARAMS,
        name="extend",
    )(me, *volumes)
    ahead = [(i, (i + 1) % slabs) for i in range(slabs)]
    behind = [(target, source) for source, target in ahead]
    before = lax.ppermute(extended, "slab", ahead)
    after = lax.ppermute(extended, "slab", behind)
    base = pl.pallas_call(
        tv_kernel,
        out_shape=jax.ShapeDtypeStruct((2, size, length), F32),
        in_specs=[VMEM, VMEM, VMEM],
        out_specs=VMEM,
        compiler_params=PARAMS,
        name="total_variation",
    )(extended, before, after)
    return (base - STEP_SIZE * jnp.concatenate(gradient, axis=1))[None]


def solution(mesh):
    placed = (
        P("slab", "coil", None, None, None),
        P("slab", "coil", None, None, None),
        P("slab", None, None),
    )
    return jax.shard_map(
        shards, mesh=mesh, in_specs=placed, out_specs=P("slab", None, "coil", None), check_vma=False
    )
```

```python
from functools import partial
import math

import jax
import jax.numpy as jnp
import ml_dtypes
import numpy as np
from jax import lax
from jax.experimental import pallas as pl
from jax.experimental.pallas import tpu as pltpu
from jax.sharding import PartitionSpec as P

STEP_SIZE = 0.25
TV_WEIGHT = 0.5
TV_SMOOTH = 0.25
CHUNKS = (5, 3)
PARTS = (2, 2)

F32 = jnp.float32
BF16 = jnp.bfloat16
VMEM = pl.BlockSpec(memory_space=pltpu.VMEM)
ANY = pl.BlockSpec(memory_space=pl.ANY)
SMEM = pl.BlockSpec(memory_space=pltpu.SMEM)
PARAMS = pltpu.CompilerParams(vmem_limit_bytes=24 * 2**20)


def dft_table(length):
    indices = np.arange(length, dtype=np.int64)
    angles = (indices[:, None] * indices[None, :] % length) * (2.0 * math.pi / length)
    factor = 1.0 / math.sqrt(length)
    table = np.concatenate([-np.sin(angles) * factor, np.cos(angles) * factor])
    return table.astype(ml_dtypes.bfloat16)


def bit_orders(count):
    top = count.bit_length() - 2
    return list(range(1, top + 1)), list(range(top, 0, -1))


def swap_cores(value):
    count = lax.axis_size("coil")
    return lax.ppermute(value, "coil", [(i, i ^ 1) for i in range(count)])


def swap_chips(value, step):
    count = lax.axis_size("coil")
    orders = bit_orders(count)
    return lax.ppermute(
        value, "coil", [(i, i ^ (1 << orders[i & 1][step])) for i in range(count)]
    )


def by_core(device, flip, values):
    return jnp.where((device & 1) ^ flip == 0, values[0], values[1])


def halving_order(steps):
    places = [0]
    for step in reversed(range(steps)):
        places = places + [place | (1 << step) for place in places]
    return places


def flops(cost):
    return pl.CostEstimate(flops=cost, bytes_accessed=4 * 2**20, transcendentals=0)


def adjoint_kernel(groups, me, table, data, sens, ready, *refs):
    del ready
    outs, (lhs, rhs) = refs[: len(groups)], refs[len(groups) :]
    length = sens.shape[1]
    device = me[0]
    blocks, at = [], 0
    for out, group in zip(outs, groups):
        for place, (start, size) in enumerate(group):
            blocks.append((out, place, at, pl.multiple_of(start(device), 16), size))
            at += size
    total = at
    for _, _, at, start, size in blocks:
        sine = table[pl.ds(start, size), :]
        cosine = table[pl.ds(pl.multiple_of(length + start, 16), size), :]
        lhs[at : at + size, :length] = cosine
        lhs[at : at + size, length:] = sine
        lhs[total + at : total + at + size, :length] = -sine
        lhs[total + at : total + at + size, length:] = cosine
    upper = jnp.dot(lhs[...], data[...], preferred_element_type=F32).astype(BF16)
    real, imag = upper[:total], upper[total:]
    rhs[:total, :length] = imag
    rhs[:total, length:] = real
    rhs[total:, :length] = -real
    rhs[total:, length:] = imag
    back = jnp.dot(rhs[...], table[...], preferred_element_type=F32)
    for out, place, at, start, size in blocks:
        rows = pl.ds(start, size)
        real, imag = back[at : at + size], back[total + at : total + at + size]
        sens_real, sens_imag = sens[0, rows, :].astype(F32), sens[1, rows, :].astype(F32)
        out[place, 0] = sens_real * real + sens_imag * imag
        out[place, 1] = sens_real * imag - sens_imag * real


def adjoint(groups, me, table, data, sens, ready=None):
    length = sens.shape[1]
    total = sum(size for group in groups for _, size in group)
    return pl.pallas_call(
        partial(adjoint_kernel, groups),
        out_shape=[
            jax.ShapeDtypeStruct((len(group), 2, group[0][1], length), F32) for group in groups
        ],
        in_specs=[SMEM, VMEM, VMEM, VMEM, ANY],
        out_specs=[VMEM] * len(groups),
        scratch_shapes=[pltpu.VMEM((2 * total, 2 * length), BF16)] * 2,
        compiler_params=PARAMS,
        cost_estimate=flops(16 * total * length * length),
        name="adjoint",
    )(me, table, data.reshape(2 * length, length), sens, me if ready is None else ready)


def columns_kernel(blocks, me, table, out, rows):
    length = out.shape[0]
    total = sum(size for _, size in blocks)
    at = 0
    for start, size in blocks:
        row = pl.multiple_of(start(me[0]), 16)
        rows[at : at + size, :] = table[pl.ds(pl.multiple_of(length + row, 16), size), :]
        rows[total + at : total + at + size, :] = table[pl.ds(row, size), :]
        at += size
    out[...] = rows[...].T


def columns(blocks, me, table):
    length = table.shape[1]
    total = 2 * sum(size for _, size in blocks)
    return pl.pallas_call(
        partial(columns_kernel, blocks),
        out_shape=jax.ShapeDtypeStruct((length, total), BF16),
        in_specs=[SMEM, VMEM],
        out_specs=VMEM,
        scratch_shapes=[pltpu.VMEM((total, length), BF16)],
        compiler_params=PARAMS,
        name="columns",
    )(me, table)


def forward_kernel(blocks, last, me, table, left, sens, *refs):
    pieces, refs = refs[: len(blocks)], refs[len(blocks) :]
    if last:
        before, kspace, sampling, out, lhs, mid = refs
    else:
        out, lhs, mid = refs
    length = sens.shape[1]
    total = sum(size for _, size in blocks)
    at = 0
    for (start, size), piece in zip(blocks, pieces):
        place = pl.ds(pl.multiple_of(start(me[0]), 16), size)
        real, imag = piece[0], piece[1]
        sens_real, sens_imag = sens[0, place, :].astype(F32), sens[1, place, :].astype(F32)
        coil_real = (sens_real * real - sens_imag * imag).astype(BF16)
        coil_imag = (sens_real * imag + sens_imag * real).astype(BF16)
        top, bottom = pl.ds(at, size), pl.ds(total + at, size)
        lhs[top, :length] = -coil_imag
        lhs[top, length:] = coil_real
        lhs[bottom, :length] = coil_real
        lhs[bottom, length:] = coil_imag
        at += size
    middle = jnp.dot(lhs[...], table[...], preferred_element_type=F32).astype(BF16)
    mid[:total, :length] = middle[:total]
    mid[:total, length:] = middle[total:]
    mid[total:, :length] = -middle[total:]
    mid[total:, length:] = middle[:total]
    freq = jnp.dot(left[...], mid[...], preferred_element_type=F32)
    if last:
        freq += before[...]
        weight = sampling[...].astype(F32)
        out[0] = (weight * (freq[:, :length] - kspace[0].astype(F32))).astype(BF16)
        out[1] = (weight * (freq[:, length:] - kspace[1].astype(F32))).astype(BF16)
    else:
        out[...] = freq


def forward(blocks, me, table, sens, pieces, rest=()):
    length = sens.shape[1]
    total = sum(size for _, size in blocks)
    left = columns(blocks, me, table)
    freq = jax.ShapeDtypeStruct((length, 2 * length), F32)
    resid = jax.ShapeDtypeStruct((2, length, length), BF16)
    return pl.pallas_call(
        partial(forward_kernel, blocks, bool(rest)),
        out_shape=resid if rest else freq,
        in_specs=[SMEM] + [VMEM] * (3 + len(pieces) + len(rest)),
        out_specs=VMEM,
        scratch_shapes=[pltpu.VMEM((2 * total, 2 * length), BF16)] * 2,
        compiler_params=PARAMS,
        cost_estimate=flops(16 * total * length * length),
        name="forward",
    )(me, table, left, sens, *pieces, *rest)


def extend_kernel(blocks, me, ready, *refs):
    del ready
    pieces, (out, volume) = refs[:-2], refs[-2:]
    length = volume.shape[1]
    own = out.shape[1] - 16
    for (start, size), piece in zip(blocks, pieces):
        volume[:, pl.ds(pl.multiple_of(start(me[0]), 16), size), :] = piece[...]
    first = me[0] * own
    for at, row, count in (
        (0, (first + length - 8) & (length - 1), 8),
        (8, first, own),
        (8 + own, (first + own) & (length - 1), 8),
    ):
        out[:, at : at + count, :] = volume[:, pl.ds(pl.multiple_of(row, 8), count), :]


def tv_kernel(own, before, after, *refs):
    out = refs[-1]
    size = out.shape[1]
    length = out.shape[2]

    def parts(ref, first, count):
        return [ref[part, first : first + count, :] for part in (0, 1)]

    def next_column(values):
        return [pltpu.roll(value, length - 1, 1) for value in values]

    def minus(left, right):
        return [a - b for a, b in zip(left, right)]

    def fluxes(here, slices, rows):
        columns = minus(next_column(here), here)
        squares = TV_SMOOTH
        for change in (slices, rows, columns):
            squares = squares + (change[0] * change[0] + change[1] * change[1])
        weight = lax.rsqrt(squares)
        return [[weight * value for value in change] for change in (slices, rows, columns)]

    count = size + 1
    here = parts(own, 7, count)
    slices, rows, columns = fluxes(
        here, minus(parts(after, 7, count), here), minus(parts(own, 8, count), here)
    )
    back = parts(before, 8, size)
    center = parts(own, 8, size)
    back_slices, _, _ = fluxes(back, minus(center, back), minus(parts(before, 9, size), back))
    for part in (0, 1):
        col = columns[part][1:]
        tv = (
            (back_slices[part] - slices[part][1:])
            + (rows[part][:-1] - rows[part][1:])
            + (pltpu.roll(col, 1, 1) - col)
        )
        out[part] = center[part] - (STEP_SIZE * TV_WEIGHT) * tv


def shards(kspace, sensitivity, sampling):
    kspace, sens, sampling = kspace[0, 0], sensitivity[0, 0], sampling[0]
    length = sampling.shape[0]
    count = lax.axis_size("coil")
    slabs = lax.axis_size("slab")
    top = count.bit_length() - 2
    size = length // count
    half = count // 2
    table = jnp.asarray(dft_table(length))
    me = lax.axis_index("coil").astype(jnp.int32).reshape(1)

    measured = kspace * sampling.astype(BF16)[None]

    orders = bit_orders(count)
    eighth = length // 8
    chunks = CHUNKS if eighth % (16 * half) == 0 or half <= 4 else (4, 4)
    chunks = [rows * eighth for rows in chunks]

    def chunk_block(chunk, flip, place):
        size = chunks[chunk] // half

        def start(device):
            own = [
                sum(((device >> bit) & 1) << step for step, bit in enumerate(order[:-1]))
                for order in orders
            ]
            block = (by_core(device, flip, own) ^ place) * 2 + ((device & 1) ^ flip)
            return sum(chunks[:chunk]) + block * size

        return start, size

    places = halving_order(top - 1)
    groups = [
        [[chunk_block(chunk, flip, place) for place in places] for chunk in range(len(chunks))]
        for flip in (1, 0)
    ]
    others = adjoint(groups[0], me, table, measured, sens)
    owns = adjoint(groups[1], me, table, measured, sens, others[0])
    currents = [own + swap_cores(other) for own, other in zip(owns, others)]
    arrived = []
    for current in currents:
        for step in range(top - 1):
            middle = current.shape[0] // 2
            current = current[:middle] + swap_chips(current[middle:], step)
        current = current[0]
        pieces = {0: current + swap_chips(current, top - 1)}
        for step in reversed(range(top - 1)):
            for place in list(pieces):
                pieces[place | (1 << step)] = swap_chips(pieces[place], step)
        arrived.append(pieces)
    early = [
        (chunk_block(chunk, flip, 0), swap_cores(pieces[0]) if flip else pieces[0])
        for chunk, pieces in enumerate(arrived)
        for flip in (0, 1)
    ]
    freq = forward([b for b, _ in early], me, table, sens, [p for _, p in early])
    late = []
    for chunk, pieces in enumerate(arrived):
        for place in range(1, half // 2):
            piece, freq = lax.optimization_barrier((pieces[place], freq))
            late.append((chunk_block(chunk, 0, place), piece))
            late.append((chunk_block(chunk, 1, place), swap_cores(piece)))
    resid = forward(
        [b for b, _ in late], me, table, sens, [p for _, p in late], [freq, kspace, sampling]
    )

    parts = [part * size // 4 for part in PARTS] if size >= 64 else [size]

    def row_block(part, flip, place):
        masks = [
            sum(((place >> step) & 1) << bit for step, bit in enumerate(order)) for order in orders
        ]
        first = sum(parts[:part])
        return (
            lambda device: (device ^ flip ^ by_core(device, flip, masks)) * size + first,
            parts[part],
        )

    places = halving_order(top)
    groups = [
        [[row_block(part, flip, place) for place in places] for part in range(len(parts))]
        for flip in (1, 0)
    ]
    others = adjoint(groups[0], me, table, resid, sens)
    owns = adjoint(groups[1], me, table, resid, sens, others[0])
    summed = [own + swap_cores(other) for own, other in zip(owns, others)]
    gradient, halves = [], []
    for current in summed:
        for step in range(top):
            middle = current.shape[0] // 2
            current = current[:middle] + swap_chips(current[middle:], step)
            halves.append(current)
        gradient.append(current[0])

    extended = pl.pallas_call(
        partial(extend_kernel, [b for b, _ in early + late]),
        out_shape=jax.ShapeDtypeStruct((2, size + 16, length), F32),
        in_specs=[SMEM, ANY] + [VMEM] * len(early + late),
        out_specs=VMEM,
        scratch_shapes=[pltpu.VMEM((2, length, length), F32)],
        compiler_params=PARAMS,
        name="extend",
    )(me, summed[-1], *[p for _, p in early + late])
    ahead = [(i, (i + 1) % slabs) for i in range(slabs)]
    behind = [(target, source) for source, target in ahead]
    before = lax.ppermute(extended, "slab", ahead)
    after = lax.ppermute(extended, "slab", behind)
    base = pl.pallas_call(
        tv_kernel,
        out_shape=jax.ShapeDtypeStruct((2, size, length), F32),
        in_specs=[VMEM, VMEM, VMEM] + [ANY] * len(parts),
        out_specs=VMEM,
        compiler_params=PARAMS,
        name="total_variation",
    )(extended, before, after, *halves[::top])
    return (base - STEP_SIZE * jnp.concatenate(gradient, axis=1))[None]


def solution(mesh):
    placed = (
        P("slab", "coil", None, None, None),
        P("slab", "coil", None, None, None),
        P("slab", None, None),
    )
    return jax.shard_map(
        shards, mesh=mesh, in_specs=placed, out_specs=P("slab", None, "coil", None), check_vma=False
    )
```

```python
from functools import partial
import math

import jax
import jax.numpy as jnp
import ml_dtypes
import numpy as np
from jax import lax
from jax.experimental import pallas as pl
from jax.experimental.pallas import tpu as pltpu
from jax.sharding import PartitionSpec as P

STEP_SIZE = 0.25
TV_WEIGHT = 0.5
TV_SMOOTH = 0.25
CHUNKS = (5, 3)
PARTS = (4,)

F32 = jnp.float32
BF16 = jnp.bfloat16
VMEM = pl.BlockSpec(memory_space=pltpu.VMEM)
ANY = pl.BlockSpec(memory_space=pl.ANY)
SMEM = pl.BlockSpec(memory_space=pltpu.SMEM)
PARAMS = pltpu.CompilerParams(vmem_limit_bytes=24 * 2**20)


def dft_table(length):
    indices = np.arange(length, dtype=np.int64)
    angles = (indices[:, None] * indices[None, :] % length) * (2.0 * math.pi / length)
    factor = 1.0 / math.sqrt(length)
    table = np.concatenate([-np.sin(angles) * factor, np.cos(angles) * factor])
    return table.astype(ml_dtypes.bfloat16)


def bit_orders(count):
    top = count.bit_length() - 2
    return list(range(1, top + 1)), list(range(top, 0, -1))


def swap_cores(value):
    count = lax.axis_size("coil")
    return lax.ppermute(value, "coil", [(i, i ^ 1) for i in range(count)])


def swap_chips(value, step):
    count = lax.axis_size("coil")
    orders = bit_orders(count)
    return lax.ppermute(
        value, "coil", [(i, i ^ (1 << orders[i & 1][step])) for i in range(count)]
    )


def by_core(device, flip, values):
    return jnp.where((device & 1) ^ flip == 0, values[0], values[1])


def halving_order(steps):
    places = [0]
    for step in reversed(range(steps)):
        places = places + [place | (1 << step) for place in places]
    return places


def flops(cost):
    return pl.CostEstimate(flops=cost, bytes_accessed=4 * 2**20, transcendentals=0)


def adjoint_kernel(groups, me, table, data, sens, ready, *refs):
    del ready
    outs, (lhs, rhs) = refs[: len(groups)], refs[len(groups) :]
    length = sens.shape[1]
    device = me[0]
    blocks, at = [], 0
    for out, group in zip(outs, groups):
        for place, (start, size) in enumerate(group):
            blocks.append((out, place, at, pl.multiple_of(start(device), 16), size))
            at += size
    total = at
    for _, _, at, start, size in blocks:
        sine = table[pl.ds(start, size), :]
        cosine = table[pl.ds(pl.multiple_of(length + start, 16), size), :]
        lhs[at : at + size, :length] = cosine
        lhs[at : at + size, length:] = sine
        lhs[total + at : total + at + size, :length] = -sine
        lhs[total + at : total + at + size, length:] = cosine
    upper = jnp.dot(lhs[...], data[...], preferred_element_type=F32).astype(BF16)
    real, imag = upper[:total], upper[total:]
    rhs[:total, :length] = imag
    rhs[:total, length:] = real
    rhs[total:, :length] = -real
    rhs[total:, length:] = imag
    back = jnp.dot(rhs[...], table[...], preferred_element_type=F32)
    for out, place, at, start, size in blocks:
        rows = pl.ds(start, size)
        real, imag = back[at : at + size], back[total + at : total + at + size]
        sens_real, sens_imag = sens[0, rows, :].astype(F32), sens[1, rows, :].astype(F32)
        out[place, 0] = sens_real * real + sens_imag * imag
        out[place, 1] = sens_real * imag - sens_imag * real


def adjoint(groups, me, table, data, sens, ready=None):
    length = sens.shape[1]
    total = sum(size for group in groups for _, size in group)
    return pl.pallas_call(
        partial(adjoint_kernel, groups),
        out_shape=[
            jax.ShapeDtypeStruct((len(group), 2, group[0][1], length), F32) for group in groups
        ],
        in_specs=[SMEM, VMEM, VMEM, VMEM, ANY],
        out_specs=[VMEM] * len(groups),
        scratch_shapes=[pltpu.VMEM((2 * total, 2 * length), BF16)] * 2,
        compiler_params=PARAMS,
        cost_estimate=flops(16 * total * length * length),
        name="adjoint",
    )(me, table, data.reshape(2 * length, length), sens, me if ready is None else ready)


def core_sums(groups, me, table, data, sens):
    halves = []
    ready = None
    for half in (1, 0):
        ours = [
            [group[half * (len(group) // 2) : (half + 1) * (len(group) // 2)] for group in part]
            for part in groups
        ]
        others = adjoint(ours[0], me, table, data, sens, ready)
        owns = adjoint(ours[1], me, table, data, sens, others[0])
        halves.append([own + swap_cores(other) for own, other in zip(owns, others)])
        ready = owns[0]
    return list(zip(halves[1], halves[0]))


def columns_kernel(groups, me, table, *refs):
    outs, rows = refs[:-1], refs[-1]
    length = table.shape[1]
    for blocks, out in zip(groups, outs):
        total = sum(size for _, size in blocks)
        at = 0
        for start, size in blocks:
            row = pl.multiple_of(start(me[0]), 16)
            rows[at : at + size, :] = table[pl.ds(pl.multiple_of(length + row, 16), size), :]
            rows[total + at : total + at + size, :] = table[pl.ds(row, size), :]
            at += size
        out[...] = rows[: 2 * total, :].T


def columns(groups, me, table):
    length = table.shape[1]
    totals = [2 * sum(size for _, size in blocks) for blocks in groups]
    return pl.pallas_call(
        partial(columns_kernel, groups),
        out_shape=[jax.ShapeDtypeStruct((length, total), BF16) for total in totals],
        in_specs=[SMEM, VMEM],
        out_specs=[VMEM] * len(groups),
        scratch_shapes=[pltpu.VMEM((max(totals), length), BF16)],
        compiler_params=PARAMS,
        name="columns",
    )(me, table)


def forward_kernel(blocks, stage, me, table, left, sens, *refs):
    pieces, refs = refs[: len(blocks)], refs[len(blocks) :]
    rest, (out, lhs, mid) = refs[:-3], refs[-3:]
    length = sens.shape[1]
    total = sum(size for _, size in blocks)
    at = 0
    for (start, size), piece in zip(blocks, pieces):
        place = pl.ds(pl.multiple_of(start(me[0]), 16), size)
        real, imag = piece[0], piece[1]
        sens_real, sens_imag = sens[0, place, :].astype(F32), sens[1, place, :].astype(F32)
        coil_real = (sens_real * real - sens_imag * imag).astype(BF16)
        coil_imag = (sens_real * imag + sens_imag * real).astype(BF16)
        top, bottom = pl.ds(at, size), pl.ds(total + at, size)
        lhs[top, :length] = -coil_imag
        lhs[top, length:] = coil_real
        lhs[bottom, :length] = coil_real
        lhs[bottom, length:] = coil_imag
        at += size
    middle = jnp.dot(lhs[...], table[...], preferred_element_type=F32).astype(BF16)
    mid[:total, :length] = middle[:total]
    mid[:total, length:] = middle[total:]
    mid[total:, :length] = -middle[total:]
    mid[total:, length:] = middle[:total]
    freq = jnp.dot(left[...], mid[...], preferred_element_type=F32)
    if stage == "first":
        (kspace,) = rest
        out[:, :length] = freq[:, :length] - kspace[0].astype(F32)
        out[:, length:] = freq[:, length:] - kspace[1].astype(F32)
    elif stage == "next":
        (before,) = rest
        out[...] = before[...] + freq
    else:
        before, mask = rest
        weight = mask[...].astype(F32)
        out[0] = (weight * (before[:, :length] + freq[:, :length])).astype(BF16)
        out[1] = (weight * (before[:, length:] + freq[:, length:])).astype(BF16)


def forward(blocks, stage, me, table, left, sens, pieces, rest):
    length = sens.shape[1]
    total = sum(size for _, size in blocks)
    freq = jax.ShapeDtypeStruct((length, 2 * length), F32)
    resid = jax.ShapeDtypeStruct((2, length, length), BF16)
    return pl.pallas_call(
        partial(forward_kernel, blocks, stage),
        out_shape=resid if stage == "last" else freq,
        in_specs=[SMEM] + [VMEM] * (3 + len(pieces) + len(rest)),
        out_specs=VMEM,
        scratch_shapes=[pltpu.VMEM((2 * total, 2 * length), BF16)] * 2,
        compiler_params=PARAMS,
        cost_estimate=flops(16 * total * length * length),
        name="forward",
    )(me, table, left, sens, *pieces, *rest)


def extend_kernel(blocks, me, ready, *refs):
    del ready
    pieces, (out, volume) = refs[:-2], refs[-2:]
    length = volume.shape[1]
    own = out.shape[1] - 16
    for (start, size), piece in zip(blocks, pieces):
        volume[:, pl.ds(pl.multiple_of(start(me[0]), 16), size), :] = piece[...]
    first = me[0] * own
    for at, row, count in (
        (0, (first + length - 8) & (length - 1), 8),
        (8, first, own),
        (8 + own, (first + own) & (length - 1), 8),
    ):
        out[:, at : at + count, :] = volume[:, pl.ds(pl.multiple_of(row, 8), count), :]


def tv_kernel(own, before, after, *refs):
    out = refs[-1]
    size = out.shape[1]
    length = out.shape[2]

    def parts(ref, first, count):
        return [ref[part, first : first + count, :] for part in (0, 1)]

    def next_column(values):
        return [pltpu.roll(value, length - 1, 1) for value in values]

    def minus(left, right):
        return [a - b for a, b in zip(left, right)]

    def fluxes(here, slices, rows):
        columns = minus(next_column(here), here)
        squares = TV_SMOOTH
        for change in (slices, rows, columns):
            squares = squares + (change[0] * change[0] + change[1] * change[1])
        weight = lax.rsqrt(squares)
        return [[weight * value for value in change] for change in (slices, rows, columns)]

    count = size + 1
    here = parts(own, 7, count)
    slices, rows, columns = fluxes(
        here, minus(parts(after, 7, count), here), minus(parts(own, 8, count), here)
    )
    back = parts(before, 8, size)
    center = parts(own, 8, size)
    back_slices, _, _ = fluxes(back, minus(center, back), minus(parts(before, 9, size), back))
    for part in (0, 1):
        col = columns[part][1:]
        tv = (
            (back_slices[part] - slices[part][1:])
            + (rows[part][:-1] - rows[part][1:])
            + (pltpu.roll(col, 1, 1) - col)
        )
        out[part] = center[part] - (STEP_SIZE * TV_WEIGHT) * tv


def shards(kspace, sensitivity, sampling):
    kspace, sens, sampling = kspace[0, 0], sensitivity[0, 0], sampling[0]
    length = sampling.shape[0]
    count = lax.axis_size("coil")
    slabs = lax.axis_size("slab")
    top = count.bit_length() - 2
    size = length // count
    half = count // 2
    table = jnp.asarray(dft_table(length))
    me = lax.axis_index("coil").astype(jnp.int32).reshape(1)

    mask = sampling.astype(BF16)
    measured = kspace * mask[None]

    orders = bit_orders(count)
    eighth = length // 8
    chunks = CHUNKS if eighth % (16 * half) == 0 or half <= 4 else (4, 4)
    chunks = [rows * eighth for rows in chunks]

    def chunk_block(chunk, flip, place):
        size = chunks[chunk] // half

        def start(device):
            own = [
                sum(((device >> bit) & 1) << step for step, bit in enumerate(order[:-1]))
                for order in orders
            ]
            block = (by_core(device, flip, own) ^ place) * 2 + ((device & 1) ^ flip)
            return sum(chunks[:chunk]) + block * size

        return start, size

    places = halving_order(top - 1)
    groups = [
        [[chunk_block(chunk, flip, place) for place in places] for chunk in range(len(chunks))]
        for flip in (1, 0)
    ]
    currents = core_sums(groups, me, table, measured, sens)
    arrived = []
    for current in currents:
        keep, send = current
        current = keep + swap_chips(send, 0)
        for step in range(1, top - 1):
            middle = current.shape[0] // 2
            current = current[:middle] + swap_chips(current[middle:], step)
        current = current[0]
        pieces = {0: current + swap_chips(current, top - 1)}
        for step in reversed(range(top - 1)):
            for place in list(pieces):
                pieces[place | (1 << step)] = swap_chips(pieces[place], step)
        arrived.append(pieces)
    early = [
        (chunk_block(chunk, flip, 0), swap_cores(pieces[0]) if flip else pieces[0])
        for chunk, pieces in enumerate(arrived)
        for flip in (0, 1)
    ]
    late_blocks = [
        [chunk_block(chunk, flip, place) for chunk in range(len(chunks)) for place in range(1, half // 2)]
        for flip in (0, 1)
    ]
    lefts = columns([[b for b, _ in early], *late_blocks], me, table)
    pieces = [p for _, p in early]
    freq = forward([b for b, _ in early], "first", me, table, lefts[0], sens, pieces, [kspace])
    late = [[], []]
    for chunk in arrived:
        for place in range(1, half // 2):
            piece, freq = lax.optimization_barrier((chunk[place], freq))
            late[0].append(piece)
            late[1].append(swap_cores(piece))
    freq = forward(late_blocks[0], "next", me, table, lefts[1], sens, late[0], [freq])
    resid = forward(late_blocks[1], "last", me, table, lefts[2], sens, late[1], [freq, mask])
    late = [*zip(late_blocks[0], late[0]), *zip(late_blocks[1], late[1])]

    parts = [part * size // 4 for part in PARTS] if size >= 64 else [size]

    def row_block(part, flip, place):
        masks = [
            sum(((place >> step) & 1) << bit for step, bit in enumerate(order)) for order in orders
        ]
        first = sum(parts[:part])
        return (
            lambda device: (device ^ flip ^ by_core(device, flip, masks)) * size + first,
            parts[part],
        )

    places = halving_order(top)
    groups = [
        [[row_block(part, flip, place) for place in places] for part in range(len(parts))]
        for flip in (1, 0)
    ]
    summed = core_sums(groups, me, table, resid, sens)
    gradient, halves = [], []
    for current in summed:
        keep, send = current
        current = keep + swap_chips(send, 0)
        halves.append(current)
        for step in range(1, top):
            middle = current.shape[0] // 2
            current = current[:middle] + swap_chips(current[middle:], step)
        gradient.append(current[0])

    extended = pl.pallas_call(
        partial(extend_kernel, [b for b, _ in early + late]),
        out_shape=jax.ShapeDtypeStruct((2, size + 16, length), F32),
        in_specs=[SMEM, ANY] + [VMEM] * len(early + late),
        out_specs=VMEM,
        scratch_shapes=[pltpu.VMEM((2, length, length), F32)],
        compiler_params=PARAMS,
        name="extend",
    )(me, summed[-1][1], *[p for _, p in early + late])
    ahead = [(i, (i + 1) % slabs) for i in range(slabs)]
    behind = [(target, source) for source, target in ahead]
    before = lax.ppermute(extended, "slab", ahead)
    after = lax.ppermute(extended, "slab", behind)
    base = pl.pallas_call(
        tv_kernel,
        out_shape=jax.ShapeDtypeStruct((2, size, length), F32),
        in_specs=[VMEM, VMEM, VMEM] + [ANY] * len(parts),
        out_specs=VMEM,
        compiler_params=PARAMS,
        name="total_variation",
    )(extended, before, after, *halves)
    return (base - STEP_SIZE * jnp.concatenate(gradient, axis=1))[None]


def solution(mesh):
    placed = (
        P("slab", "coil", None, None, None),
        P("slab", "coil", None, None, None),
        P("slab", None, None),
    )
    return jax.shard_map(
        shards, mesh=mesh, in_specs=placed, out_specs=P("slab", None, "coil", None), check_vma=False
    )
```

```python
from functools import partial
import math

import jax
import jax.numpy as jnp
import ml_dtypes
import numpy as np
from jax import lax
from jax.experimental import pallas as pl
from jax.experimental.pallas import tpu as pltpu
from jax.sharding import PartitionSpec as P

STEP_SIZE = 0.25
TV_WEIGHT = 0.5
TV_SMOOTH = 0.25
CHUNKS = (5, 3)

F32 = jnp.float32
BF16 = jnp.bfloat16
VMEM = pl.BlockSpec(memory_space=pltpu.VMEM)
ANY = pl.BlockSpec(memory_space=pl.ANY)
SMEM = pl.BlockSpec(memory_space=pltpu.SMEM)
PARAMS = pltpu.CompilerParams(vmem_limit_bytes=24 * 2**20)


def dft_table(length):
    indices = np.arange(length, dtype=np.int64)
    angles = (indices[:, None] * indices[None, :] % length) * (2.0 * math.pi / length)
    factor = 1.0 / math.sqrt(length)
    table = np.concatenate([-np.sin(angles) * factor, np.cos(angles) * factor])
    return table.astype(ml_dtypes.bfloat16)


def bit_orders(count):
    top = count.bit_length() - 2
    return list(range(1, top + 1)), list(range(top, 0, -1))


def swap_cores(value):
    count = lax.axis_size("coil")
    return lax.ppermute(value, "coil", [(i, i ^ 1) for i in range(count)])


def swap_chips(value, step):
    count = lax.axis_size("coil")
    orders = bit_orders(count)
    return lax.ppermute(
        value, "coil", [(i, i ^ (1 << orders[i & 1][step])) for i in range(count)]
    )


def by_core(device, flip, values):
    return jnp.where((device & 1) ^ flip == 0, values[0], values[1])


def halving_order(steps):
    places = [0]
    for step in reversed(range(steps)):
        places = places + [place | (1 << step) for place in places]
    return places


def flops(cost):
    return pl.CostEstimate(flops=cost, bytes_accessed=4 * 2**20, transcendentals=0)


def adjoint_kernel(groups, me, table, data, sens, ready, *refs):
    del ready
    outs, (lhs, rhs) = refs[: len(groups)], refs[len(groups) :]
    length = sens.shape[1]
    device = me[0]
    blocks, at = [], 0
    for out, group in zip(outs, groups):
        for place, (start, size) in enumerate(group):
            blocks.append((out, place, at, pl.multiple_of(start(device), 16), size))
            at += size
    total = at
    for _, _, at, start, size in blocks:
        sine = table[pl.ds(start, size), :]
        cosine = table[pl.ds(pl.multiple_of(length + start, 16), size), :]
        lhs[at : at + size, :length] = cosine
        lhs[at : at + size, length:] = sine
        lhs[total + at : total + at + size, :length] = -sine
        lhs[total + at : total + at + size, length:] = cosine
    upper = jnp.dot(lhs[...], data[...], preferred_element_type=F32).astype(BF16)
    real, imag = upper[:total], upper[total:]
    rhs[:total, :length] = imag
    rhs[:total, length:] = real
    rhs[total:, :length] = -real
    rhs[total:, length:] = imag
    back = jnp.dot(rhs[...], table[...], preferred_element_type=F32)
    for out, place, at, start, size in blocks:
        rows = pl.ds(start, size)
        real, imag = back[at : at + size], back[total + at : total + at + size]
        sens_real, sens_imag = sens[0, rows, :].astype(F32), sens[1, rows, :].astype(F32)
        out[place, 0] = sens_real * real + sens_imag * imag
        out[place, 1] = sens_real * imag - sens_imag * real


def adjoint(groups, me, table, data, sens, ready=None):
    length = sens.shape[1]
    total = sum(size for group in groups for _, size in group)
    return pl.pallas_call(
        partial(adjoint_kernel, groups),
        out_shape=[
            jax.ShapeDtypeStruct((len(group), 2, group[0][1], length), F32) for group in groups
        ],
        in_specs=[SMEM, VMEM, VMEM, VMEM, ANY],
        out_specs=[VMEM] * len(groups),
        scratch_shapes=[pltpu.VMEM((2 * total, 2 * length), BF16)] * 2,
        compiler_params=PARAMS,
        cost_estimate=flops(16 * total * length * length),
        name="adjoint",
    )(me, table, data.reshape(2 * length, length), sens, me if ready is None else ready)


def core_sums(groups, me, table, data, sens):
    halves = []
    ready = None
    for half in (1, 0):
        ours = [
            [group[half * (len(group) // 2) : (half + 1) * (len(group) // 2)] for group in part]
            for part in groups
        ]
        others = adjoint(ours[0], me, table, data, sens, ready)
        owns = adjoint(ours[1], me, table, data, sens, others[0])
        halves.append([own + swap_cores(other) for own, other in zip(owns, others)])
        ready = owns[0]
    return list(zip(halves[1], halves[0]))


def columns_kernel(groups, me, table, *refs):
    outs, rows = refs[:-1], refs[-1]
    length = table.shape[1]
    for blocks, out in zip(groups, outs):
        total = sum(size for _, size in blocks)
        at = 0
        for start, size in blocks:
            row = pl.multiple_of(start(me[0]), 16)
            rows[at : at + size, :] = table[pl.ds(pl.multiple_of(length + row, 16), size), :]
            rows[total + at : total + at + size, :] = table[pl.ds(row, size), :]
            at += size
        out[...] = rows[: 2 * total, :].T


def columns(groups, me, table):
    length = table.shape[1]
    totals = [2 * sum(size for _, size in blocks) for blocks in groups]
    return pl.pallas_call(
        partial(columns_kernel, groups),
        out_shape=[jax.ShapeDtypeStruct((length, total), BF16) for total in totals],
        in_specs=[SMEM, VMEM],
        out_specs=[VMEM] * len(groups),
        scratch_shapes=[pltpu.VMEM((max(totals), length), BF16)],
        compiler_params=PARAMS,
        name="columns",
    )(me, table)


def forward_kernel(blocks, stage, me, table, left, sens, *refs):
    pieces, refs = refs[: len(blocks)], refs[len(blocks) :]
    rest, (out, lhs, mid) = refs[:-3], refs[-3:]
    length = sens.shape[1]
    total = sum(size for _, size in blocks)
    at = 0
    for (start, size), piece in zip(blocks, pieces):
        place = pl.ds(pl.multiple_of(start(me[0]), 16), size)
        real, imag = piece[0], piece[1]
        sens_real, sens_imag = sens[0, place, :].astype(F32), sens[1, place, :].astype(F32)
        coil_real = (sens_real * real - sens_imag * imag).astype(BF16)
        coil_imag = (sens_real * imag + sens_imag * real).astype(BF16)
        top, bottom = pl.ds(at, size), pl.ds(total + at, size)
        lhs[top, :length] = -coil_imag
        lhs[top, length:] = coil_real
        lhs[bottom, :length] = coil_real
        lhs[bottom, length:] = coil_imag
        at += size
    middle = jnp.dot(lhs[...], table[...], preferred_element_type=F32).astype(BF16)
    mid[:total, :length] = middle[:total]
    mid[:total, length:] = middle[total:]
    mid[total:, :length] = -middle[total:]
    mid[total:, length:] = middle[:total]
    freq = jnp.dot(left[...], mid[...], preferred_element_type=F32)
    if stage == "first":
        (kspace,) = rest
        out[:, :length] = freq[:, :length] - kspace[0].astype(F32)
        out[:, length:] = freq[:, length:] - kspace[1].astype(F32)
    elif stage == "next":
        (before,) = rest
        out[...] = before[...] + freq
    else:
        before, mask = rest
        weight = mask[...].astype(F32)
        out[0] = (weight * (before[:, :length] + freq[:, :length])).astype(BF16)
        out[1] = (weight * (before[:, length:] + freq[:, length:])).astype(BF16)


def forward(blocks, stage, me, table, left, sens, pieces, rest):
    length = sens.shape[1]
    total = sum(size for _, size in blocks)
    freq = jax.ShapeDtypeStruct((length, 2 * length), F32)
    resid = jax.ShapeDtypeStruct((2, length, length), BF16)
    return pl.pallas_call(
        partial(forward_kernel, blocks, stage),
        out_shape=resid if stage == "last" else freq,
        in_specs=[SMEM] + [VMEM] * (3 + len(pieces) + len(rest)),
        out_specs=VMEM,
        scratch_shapes=[pltpu.VMEM((2 * total, 2 * length), BF16)] * 2,
        compiler_params=PARAMS,
        cost_estimate=flops(16 * total * length * length),
        name="forward",
    )(me, table, left, sens, *pieces, *rest)


def extend_kernel(blocks, me, *refs):
    pieces, (out, to_before, to_after, volume) = refs[:-4], refs[-4:]
    length = volume.shape[1]
    own = out.shape[1] - 16
    for (start, size), piece in zip(blocks, pieces):
        volume[:, pl.ds(pl.multiple_of(start(me[0]), 16), size), :] = piece[...]
    first = me[0] * own
    for at, row, count in (
        (0, (first + length - 8) & (length - 1), 8),
        (8, first, own),
        (8 + own, (first + own) & (length - 1), 8),
    ):
        values = volume[:, pl.ds(pl.multiple_of(row, 8), count), :]
        out[:, at : at + count, :] = values
        if at <= 8:
            to_before[:, at : at + count, :] = values
        if at >= 8:
            to_after[:, at - 8 : at - 8 + count, :] = values


def tv_kernel(own, before, after, kept, arrived, out):
    size = out.shape[1]
    length = out.shape[2]

    def parts(ref, first, count):
        return [ref[part, first : first + count, :] for part in (0, 1)]

    def next_column(values):
        return [pltpu.roll(value, length - 1, 1) for value in values]

    def minus(left, right):
        return [a - b for a, b in zip(left, right)]

    def fluxes(here, slices, rows):
        columns = minus(next_column(here), here)
        squares = TV_SMOOTH
        for change in (slices, rows, columns):
            squares = squares + (change[0] * change[0] + change[1] * change[1])
        weight = lax.rsqrt(squares)
        return [[weight * value for value in change] for change in (slices, rows, columns)]

    count = size + 1
    here = parts(own, 7, count)
    slices, rows, columns = fluxes(
        here, minus(parts(after, 7, count), here), minus(parts(own, 8, count), here)
    )
    back = parts(before, 0, size)
    center = parts(own, 8, size)
    back_slices, _, _ = fluxes(back, minus(center, back), minus(parts(before, 1, size), back))
    for part in (0, 1):
        col = columns[part][1:]
        tv = (
            (back_slices[part] - slices[part][1:])
            + (rows[part][:-1] - rows[part][1:])
            + (pltpu.roll(col, 1, 1) - col)
        )
        gradient = kept[0, part] + arrived[0, part]
        out[part] = center[part] - STEP_SIZE * (gradient + TV_WEIGHT * tv)


def shards(kspace, sensitivity, sampling):
    kspace, sens, sampling = kspace[0, 0], sensitivity[0, 0], sampling[0]
    length = sampling.shape[0]
    count = lax.axis_size("coil")
    slabs = lax.axis_size("slab")
    top = count.bit_length() - 2
    size = length // count
    half = count // 2
    table = jnp.asarray(dft_table(length))
    me = lax.axis_index("coil").astype(jnp.int32).reshape(1)

    mask = sampling.astype(BF16)
    measured = kspace * mask[None]

    orders = bit_orders(count)
    eighth = length // 8
    chunks = CHUNKS if eighth % (16 * half) == 0 or half <= 4 else (4, 4)
    chunks = [rows * eighth for rows in chunks]

    def chunk_block(chunk, flip, place):
        size = chunks[chunk] // half

        def start(device):
            own = [
                sum(((device >> bit) & 1) << step for step, bit in enumerate(order[:-1]))
                for order in orders
            ]
            block = (by_core(device, flip, own) ^ place) * 2 + ((device & 1) ^ flip)
            return sum(chunks[:chunk]) + block * size

        return start, size

    places = halving_order(top - 1)
    groups = [
        [[chunk_block(chunk, flip, place) for place in places] for chunk in range(len(chunks))]
        for flip in (1, 0)
    ]
    currents = core_sums(groups, me, table, measured, sens)
    arrived = []
    for current in currents:
        keep, send = current
        current = keep + swap_chips(send, 0)
        for step in range(1, top - 1):
            middle = current.shape[0] // 2
            current = current[:middle] + swap_chips(current[middle:], step)
        current = current[0]
        pieces = {0: current + swap_chips(current, top - 1)}
        for step in reversed(range(top - 1)):
            for place in list(pieces):
                pieces[place | (1 << step)] = swap_chips(pieces[place], step)
        arrived.append(pieces)
    early = [
        (chunk_block(chunk, flip, 0), swap_cores(pieces[0]) if flip else pieces[0])
        for chunk, pieces in enumerate(arrived)
        for flip in (0, 1)
    ]
    late_blocks = [
        [chunk_block(chunk, flip, place) for chunk in range(len(chunks)) for place in range(1, half // 2)]
        for flip in (0, 1)
    ]
    lefts = columns([[b for b, _ in early], *late_blocks], me, table)
    pieces = [p for _, p in early]
    freq = forward([b for b, _ in early], "first", me, table, lefts[0], sens, pieces, [kspace])
    late = [[], []]
    for chunk in arrived:
        for place in range(1, half // 2):
            piece, freq = lax.optimization_barrier((chunk[place], freq))
            late[0].append(piece)
            late[1].append(swap_cores(piece))
    freq = forward(late_blocks[0], "next", me, table, lefts[1], sens, late[0], [freq])
    resid = forward(late_blocks[1], "last", me, table, lefts[2], sens, late[1], [freq, mask])
    late = [*zip(late_blocks[0], late[0]), *zip(late_blocks[1], late[1])]

    parts = [size]

    def row_block(part, flip, place):
        masks = [
            sum(((place >> step) & 1) << bit for step, bit in enumerate(order)) for order in orders
        ]
        first = sum(parts[:part])
        return (
            lambda device: (device ^ flip ^ by_core(device, flip, masks)) * size + first,
            parts[part],
        )

    places = halving_order(top)
    groups = [
        [[row_block(part, flip, place) for place in places] for part in range(len(parts))]
        for flip in (1, 0)
    ]
    summed = core_sums(groups, me, table, resid, sens)
    keep, send = summed[0]
    for step in range(top - 1):
        middle = keep.shape[0] // 2
        passed = keep[middle:] + swap_chips(send[middle:], step)
        kept = [keep[:middle], swap_chips(send[:middle], step)]
        if step < top - 2:
            keep = kept[0] + kept[1]
        send = passed
    gradient = swap_chips(send, top - 1)

    extended, to_before, to_after = pl.pallas_call(
        partial(extend_kernel, [b for b, _ in early + late]),
        out_shape=[jax.ShapeDtypeStruct((2, size + more, length), F32) for more in (16, 8, 8)],
        in_specs=[SMEM] + [VMEM] * len(early + late),
        out_specs=[VMEM] * 3,
        scratch_shapes=[pltpu.VMEM((2, length, length), F32)],
        compiler_params=PARAMS,
        name="extend",
    )(me, *[p for _, p in early + late])
    ahead = [(i, (i + 1) % slabs) for i in range(slabs)]
    behind = [(target, source) for source, target in ahead]
    before = lax.ppermute(to_after, "slab", ahead)
    after = lax.ppermute(to_before, "slab", behind)
    base = pl.pallas_call(
        tv_kernel,
        out_shape=jax.ShapeDtypeStruct((2, size, length), F32),
        in_specs=[VMEM] * 5,
        out_specs=VMEM,
        compiler_params=PARAMS,
        name="total_variation",
    )(extended, before, after, *kept)
    return (base - STEP_SIZE * gradient[0])[None]


def solution(mesh):
    placed = (
        P("slab", "coil", None, None, None),
        P("slab", "coil", None, None, None),
        P("slab", None, None),
    )
    return jax.shard_map(
        shards, mesh=mesh, in_specs=placed, out_specs=P("slab", None, "coil", None), check_vma=False
    )
```

```python
from functools import partial
import math

import jax
import jax.numpy as jnp
import ml_dtypes
import numpy as np
from jax import lax
from jax.experimental import pallas as pl
from jax.experimental.pallas import tpu as pltpu
from jax.sharding import PartitionSpec as P

STEP_SIZE = 0.25
TV_WEIGHT = 0.5
TV_SMOOTH = 0.25
CHUNKS = (5, 3)

F32 = jnp.float32
BF16 = jnp.bfloat16
VMEM = pl.BlockSpec(memory_space=pltpu.VMEM)
ANY = pl.BlockSpec(memory_space=pl.ANY)
SMEM = pl.BlockSpec(memory_space=pltpu.SMEM)
PARAMS = pltpu.CompilerParams(vmem_limit_bytes=24 * 2**20)


def dft_table(length):
    indices = np.arange(length, dtype=np.int64)
    angles = (indices[:, None] * indices[None, :] % length) * (2.0 * math.pi / length)
    factor = 1.0 / math.sqrt(length)
    table = np.concatenate([-np.sin(angles) * factor, np.cos(angles) * factor])
    return table.astype(ml_dtypes.bfloat16)


def bit_orders(count):
    top = count.bit_length() - 2
    return list(range(1, top + 1)), list(range(top, 0, -1))


def swap_cores(value):
    count = lax.axis_size("coil")
    return lax.ppermute(value, "coil", [(i, i ^ 1) for i in range(count)])


def swap_chips(value, step):
    count = lax.axis_size("coil")
    orders = bit_orders(count)
    return lax.ppermute(
        value, "coil", [(i, i ^ (1 << orders[i & 1][step])) for i in range(count)]
    )


def by_core(device, flip, values):
    return jnp.where((device & 1) ^ flip == 0, values[0], values[1])


def halving_order(steps):
    places = [0]
    for step in reversed(range(steps)):
        places = places + [place | (1 << step) for place in places]
    return places


def flops(cost):
    return pl.CostEstimate(flops=cost, bytes_accessed=4 * 2**20, transcendentals=0)


def adjoint_kernel(groups, me, table, data, sens, ready, *refs):
    del ready
    outs, (lhs, rhs) = refs[: len(groups)], refs[len(groups) :]
    length = sens.shape[1]
    device = me[0]
    blocks, at = [], 0
    for out, group in zip(outs, groups):
        for place, (start, size) in enumerate(group):
            blocks.append((out, place, at, pl.multiple_of(start(device), 16), size))
            at += size
    total = at
    for _, _, at, start, size in blocks:
        sine = table[pl.ds(start, size), :]
        cosine = table[pl.ds(pl.multiple_of(length + start, 16), size), :]
        lhs[at : at + size, :length] = cosine
        lhs[at : at + size, length:] = sine
        lhs[total + at : total + at + size, :length] = -sine
        lhs[total + at : total + at + size, length:] = cosine
    upper = jnp.dot(lhs[...], data[...], preferred_element_type=F32).astype(BF16)
    real, imag = upper[:total], upper[total:]
    rhs[:total, :length] = imag
    rhs[:total, length:] = real
    rhs[total:, :length] = -real
    rhs[total:, length:] = imag
    back = jnp.dot(rhs[...], table[...], preferred_element_type=F32)
    for out, place, at, start, size in blocks:
        rows = pl.ds(start, size)
        real, imag = back[at : at + size], back[total + at : total + at + size]
        sens_real, sens_imag = sens[0, rows, :].astype(F32), sens[1, rows, :].astype(F32)
        out[place, 0] = sens_real * real + sens_imag * imag
        out[place, 1] = sens_real * imag - sens_imag * real


def adjoint(groups, me, table, data, sens, ready=None):
    length = sens.shape[1]
    total = sum(size for group in groups for _, size in group)
    return pl.pallas_call(
        partial(adjoint_kernel, groups),
        out_shape=[
            jax.ShapeDtypeStruct((len(group), 2, group[0][1], length), F32) for group in groups
        ],
        in_specs=[SMEM, VMEM, VMEM, VMEM, ANY],
        out_specs=[VMEM] * len(groups),
        scratch_shapes=[pltpu.VMEM((2 * total, 2 * length), BF16)] * 2,
        compiler_params=PARAMS,
        cost_estimate=flops(16 * total * length * length),
        name="adjoint",
    )(me, table, data.reshape(2 * length, length), sens, me if ready is None else ready)


def core_sums(plan, me, table, data, sens):
    terms, ready = {}, None
    for groups in plan:
        results = adjoint([blocks for _, _, blocks in groups], me, table, data, sens, ready)
        terms.update(((name, flip), value) for (name, flip, _), value in zip(groups, results))
        ready = results[0]
    names = [name for name, flip in terms if flip]
    return {name: terms[name, 0] + swap_cores(terms[name, 1]) for name in names}


def columns_kernel(groups, me, table, *refs):
    outs, rows = refs[:-1], refs[-1]
    length = table.shape[1]
    for blocks, out in zip(groups, outs):
        total = sum(size for _, size in blocks)
        at = 0
        for start, size in blocks:
            row = pl.multiple_of(start(me[0]), 16)
            rows[at : at + size, :] = table[pl.ds(pl.multiple_of(length + row, 16), size), :]
            rows[total + at : total + at + size, :] = table[pl.ds(row, size), :]
            at += size
        out[...] = rows[: 2 * total, :].T


def columns(groups, me, table):
    length = table.shape[1]
    totals = [2 * sum(size for _, size in blocks) for blocks in groups]
    return pl.pallas_call(
        partial(columns_kernel, groups),
        out_shape=[jax.ShapeDtypeStruct((length, total), BF16) for total in totals],
        in_specs=[SMEM, VMEM],
        out_specs=[VMEM] * len(groups),
        scratch_shapes=[pltpu.VMEM((max(totals), length), BF16)],
        compiler_params=PARAMS,
        name="columns",
    )(me, table)


def forward_kernel(blocks, stage, me, table, left, sens, *refs):
    pieces, refs = refs[: len(blocks)], refs[len(blocks) :]
    rest, (out, lhs, mid) = refs[:-3], refs[-3:]
    length = sens.shape[1]
    total = sum(size for _, size in blocks)
    at = 0
    for (start, size), piece in zip(blocks, pieces):
        place = pl.ds(pl.multiple_of(start(me[0]), 16), size)
        real, imag = piece[0], piece[1]
        sens_real, sens_imag = sens[0, place, :].astype(F32), sens[1, place, :].astype(F32)
        coil_real = (sens_real * real - sens_imag * imag).astype(BF16)
        coil_imag = (sens_real * imag + sens_imag * real).astype(BF16)
        top, bottom = pl.ds(at, size), pl.ds(total + at, size)
        lhs[top, :length] = -coil_imag
        lhs[top, length:] = coil_real
        lhs[bottom, :length] = coil_real
        lhs[bottom, length:] = coil_imag
        at += size
    middle = jnp.dot(lhs[...], table[...], preferred_element_type=F32).astype(BF16)
    mid[:total, :length] = middle[:total]
    mid[:total, length:] = middle[total:]
    mid[total:, :length] = -middle[total:]
    mid[total:, length:] = middle[:total]
    freq = jnp.dot(left[...], mid[...], preferred_element_type=F32)
    if stage == "first":
        (kspace,) = rest
        out[:, :length] = freq[:, :length] - kspace[0].astype(F32)
        out[:, length:] = freq[:, length:] - kspace[1].astype(F32)
    elif stage == "next":
        (before,) = rest
        out[...] = before[...] + freq
    else:
        before, mask = rest
        weight = mask[...].astype(F32)
        out[0] = (weight * (before[:, :length] + freq[:, :length])).astype(BF16)
        out[1] = (weight * (before[:, length:] + freq[:, length:])).astype(BF16)


def forward(blocks, stage, me, table, left, sens, pieces, rest):
    length = sens.shape[1]
    total = sum(size for _, size in blocks)
    freq = jax.ShapeDtypeStruct((length, 2 * length), F32)
    resid = jax.ShapeDtypeStruct((2, length, length), BF16)
    return pl.pallas_call(
        partial(forward_kernel, blocks, stage),
        out_shape=resid if stage == "last" else freq,
        in_specs=[SMEM] + [VMEM] * (3 + len(pieces) + len(rest)),
        out_specs=VMEM,
        scratch_shapes=[pltpu.VMEM((2 * total, 2 * length), BF16)] * 2,
        compiler_params=PARAMS,
        cost_estimate=flops(16 * total * length * length),
        name="forward",
    )(me, table, left, sens, *pieces, *rest)


def extend_kernel(blocks, me, *refs):
    pieces, (out, to_before, to_after, volume) = refs[:-4], refs[-4:]
    length = volume.shape[1]
    own = out.shape[1] - 16
    for (start, size), piece in zip(blocks, pieces):
        volume[:, pl.ds(pl.multiple_of(start(me[0]), 16), size), :] = piece[...]
    first = me[0] * own
    for at, row, count in (
        (0, (first + length - 8) & (length - 1), 8),
        (8, first, own),
        (8 + own, (first + own) & (length - 1), 8),
    ):
        values = volume[:, pl.ds(pl.multiple_of(row, 8), count), :]
        out[:, at : at + count, :] = values
        if at <= 8:
            to_before[:, at : at + count, :] = values
        if at >= 8:
            to_after[:, at - 8 : at - 8 + count, :] = values


def tv_kernel(own, before, after, kept, arrived, out):
    size = out.shape[1]
    length = out.shape[2]

    def parts(ref, first, count):
        return [ref[part, first : first + count, :] for part in (0, 1)]

    def next_column(values):
        return [pltpu.roll(value, length - 1, 1) for value in values]

    def minus(left, right):
        return [a - b for a, b in zip(left, right)]

    def fluxes(here, slices, rows):
        columns = minus(next_column(here), here)
        squares = TV_SMOOTH
        for change in (slices, rows, columns):
            squares = squares + (change[0] * change[0] + change[1] * change[1])
        weight = lax.rsqrt(squares)
        return [[weight * value for value in change] for change in (slices, rows, columns)]

    count = size + 1
    here = parts(own, 7, count)
    slices, rows, columns = fluxes(
        here, minus(parts(after, 7, count), here), minus(parts(own, 8, count), here)
    )
    back = parts(before, 0, size)
    center = parts(own, 8, size)
    back_slices, _, _ = fluxes(back, minus(center, back), minus(parts(before, 1, size), back))
    for part in (0, 1):
        col = columns[part][1:]
        tv = (
            (back_slices[part] - slices[part][1:])
            + (rows[part][:-1] - rows[part][1:])
            + (pltpu.roll(col, 1, 1) - col)
        )
        gradient = kept[0, part] + arrived[0, part]
        out[part] = center[part] - STEP_SIZE * (gradient + TV_WEIGHT * tv)


def shards(kspace, sensitivity, sampling):
    kspace, sens, sampling = kspace[0, 0], sensitivity[0, 0], sampling[0]
    length = sampling.shape[0]
    count = lax.axis_size("coil")
    slabs = lax.axis_size("slab")
    top = count.bit_length() - 2
    size = length // count
    half = count // 2
    table = jnp.asarray(dft_table(length))
    me = lax.axis_index("coil").astype(jnp.int32).reshape(1)

    mask = sampling.astype(BF16)
    measured = kspace * mask[None]

    orders = bit_orders(count)
    eighth = length // 8
    chunks = CHUNKS if eighth % (16 * half) == 0 or half <= 4 else (4, 4)
    chunks = [rows * eighth for rows in chunks]

    def chunk_block(chunk, flip, place):
        size = chunks[chunk] // half

        def start(device):
            own = [
                sum(((device >> bit) & 1) << step for step, bit in enumerate(order[:-1]))
                for order in orders
            ]
            block = (by_core(device, flip, own) ^ place) * 2 + ((device & 1) ^ flip)
            return sum(chunks[:chunk]) + block * size

        return start, size

    places = halving_order(top - 1)
    middle = len(places) // 2
    sent, kept = [], []
    for chunk in range(len(chunks)):
        blocks = [[chunk_block(chunk, flip, place) for place in places] for flip in (0, 1)]
        sent.append([(("send", chunk), flip, blocks[flip][middle:]) for flip in (0, 1)])
        kept.append([(("keep", chunk), flip, blocks[flip][:middle]) for flip in (0, 1)])
    plan = [
        [sent[0][1]],
        [sent[0][0]] + [own_other[1] for own_other in sent[1:] + kept],
        [own_other[0] for own_other in sent[1:] + kept],
    ]
    sums = core_sums(plan, me, table, measured, sens)
    currents = [(sums["keep", chunk], sums["send", chunk]) for chunk in range(len(chunks))]
    arrived = []
    for current in currents:
        keep, send = current
        current = keep + swap_chips(send, 0)
        for step in range(1, top - 1):
            middle = current.shape[0] // 2
            current = current[:middle] + swap_chips(current[middle:], step)
        current = current[0]
        pieces = {0: current + swap_chips(current, top - 1)}
        for step in reversed(range(top - 1)):
            for place in list(pieces):
                pieces[place | (1 << step)] = swap_chips(pieces[place], step)
        arrived.append(pieces)
    early = [
        (chunk_block(chunk, flip, 0), swap_cores(pieces[0]) if flip else pieces[0])
        for chunk, pieces in enumerate(arrived)
        for flip in (0, 1)
    ]
    late_blocks = [
        [chunk_block(chunk, flip, place) for chunk in range(len(chunks)) for place in range(1, half // 2)]
        for flip in (0, 1)
    ]
    lefts = columns([[b for b, _ in early], *late_blocks], me, table)
    pieces = [p for _, p in early]
    freq = forward([b for b, _ in early], "first", me, table, lefts[0], sens, pieces, [kspace])
    late = [[], []]
    for chunk in arrived:
        for place in range(1, half // 2):
            piece, freq = lax.optimization_barrier((chunk[place], freq))
            late[0].append(piece)
            late[1].append(swap_cores(piece))
    freq = forward(late_blocks[0], "next", me, table, lefts[1], sens, late[0], [freq])
    resid = forward(late_blocks[1], "last", me, table, lefts[2], sens, late[1], [freq, mask])
    late = [*zip(late_blocks[0], late[0]), *zip(late_blocks[1], late[1])]

    parts = [size]

    def row_block(part, flip, place):
        masks = [
            sum(((place >> step) & 1) << bit for step, bit in enumerate(order)) for order in orders
        ]
        first = sum(parts[:part])
        return (
            lambda device: (device ^ flip ^ by_core(device, flip, masks)) * size + first,
            parts[part],
        )

    places = halving_order(top)
    blocks = [[row_block(0, flip, place) for place in places] for flip in (0, 1)]
    middle, quarter = len(places) // 2, len(places) // 4
    passed = [("passed", flip, blocks[flip][middle + quarter :]) for flip in (0, 1)]
    stays = [("stays", flip, blocks[flip][middle : middle + quarter]) for flip in (0, 1)]
    kept = [("keep", flip, blocks[flip][:middle]) for flip in (0, 1)]
    both = [("send", flip, blocks[flip][middle:]) for flip in (0, 1)]
    plan = [[both[1]], [both[0], kept[1]], [kept[0]]]
    sums = core_sums(plan, me, table, resid, sens)
    keep, passed, stays = sums["keep"], sums["send"][quarter:], sums["send"][:quarter]
    for step in range(top - 1):
        middle = keep.shape[0] // 2
        if step:
            passed, stays = send[middle:], send[:middle]
        send = keep[middle:] + swap_chips(passed, step)
        kept = [keep[:middle], swap_chips(stays, step)]
        if step < top - 2:
            keep = kept[0] + kept[1]
    gradient = swap_chips(send, top - 1)

    extended, to_before, to_after = pl.pallas_call(
        partial(extend_kernel, [b for b, _ in early + late]),
        out_shape=[jax.ShapeDtypeStruct((2, size + more, length), F32) for more in (16, 8, 8)],
        in_specs=[SMEM] + [VMEM] * len(early + late),
        out_specs=[VMEM] * 3,
        scratch_shapes=[pltpu.VMEM((2, length, length), F32)],
        compiler_params=PARAMS,
        name="extend",
    )(me, *[p for _, p in early + late])
    ahead = [(i, (i + 1) % slabs) for i in range(slabs)]
    behind = [(target, source) for source, target in ahead]
    before = lax.ppermute(to_after, "slab", ahead)
    after = lax.ppermute(to_before, "slab", behind)
    base = pl.pallas_call(
        tv_kernel,
        out_shape=jax.ShapeDtypeStruct((2, size, length), F32),
        in_specs=[VMEM] * 5,
        out_specs=VMEM,
        compiler_params=PARAMS,
        name="total_variation",
    )(extended, before, after, *kept)
    return (base - STEP_SIZE * gradient[0])[None]


def solution(mesh):
    placed = (
        P("slab", "coil", None, None, None),
        P("slab", "coil", None, None, None),
        P("slab", None, None),
    )
    return jax.shard_map(
        shards, mesh=mesh, in_specs=placed, out_specs=P("slab", None, "coil", None), check_vma=False
    )
```

```python
from functools import partial
import math

import jax
import jax.numpy as jnp
import ml_dtypes
import numpy as np
from jax import lax
from jax.experimental import pallas as pl
from jax.experimental.pallas import tpu as pltpu
from jax.sharding import PartitionSpec as P

STEP_SIZE = 0.25
TV_WEIGHT = 0.5
TV_SMOOTH = 0.25
CHUNKS = (5, 3)

F32 = jnp.float32
BF16 = jnp.bfloat16
VMEM = pl.BlockSpec(memory_space=pltpu.VMEM)
ANY = pl.BlockSpec(memory_space=pl.ANY)
SMEM = pl.BlockSpec(memory_space=pltpu.SMEM)
PARAMS = pltpu.CompilerParams(vmem_limit_bytes=24 * 2**20)


def dft_table(length):
    indices = np.arange(length, dtype=np.int64)
    angles = (indices[:, None] * indices[None, :] % length) * (2.0 * math.pi / length)
    factor = 1.0 / math.sqrt(length)
    table = np.concatenate([-np.sin(angles) * factor, np.cos(angles) * factor])
    return table.astype(ml_dtypes.bfloat16)


def bit_orders(count):
    top = count.bit_length() - 2
    return list(range(1, top + 1)), list(range(top, 0, -1))


def swap_cores(value):
    count = lax.axis_size("coil")
    return lax.ppermute(value, "coil", [(i, i ^ 1) for i in range(count)])


def swap_chips(value, step):
    count = lax.axis_size("coil")
    orders = bit_orders(count)
    return lax.ppermute(
        value, "coil", [(i, i ^ (1 << orders[i & 1][step])) for i in range(count)]
    )


def by_core(device, flip, values):
    return jnp.where((device & 1) ^ flip == 0, values[0], values[1])


def halving_order(steps):
    places = [0]
    for step in reversed(range(steps)):
        places = places + [place | (1 << step) for place in places]
    return places


def flops(cost):
    return pl.CostEstimate(flops=cost, bytes_accessed=4 * 2**20, transcendentals=0)


def adjoint_kernel(groups, me, table, data, sens, ready, *refs):
    del ready
    outs, (lhs, rhs) = refs[: len(groups)], refs[len(groups) :]
    length = sens.shape[1]
    device = me[0]
    blocks, at = [], 0
    for out, group in zip(outs, groups):
        for place, (start, size) in enumerate(group):
            blocks.append((out, place, at, pl.multiple_of(start(device), 16), size))
            at += size
    total = at
    for _, _, at, start, size in blocks:
        sine = table[pl.ds(start, size), :]
        cosine = table[pl.ds(pl.multiple_of(length + start, 16), size), :]
        lhs[at : at + size, :length] = cosine
        lhs[at : at + size, length:] = sine
        lhs[total + at : total + at + size, :length] = -sine
        lhs[total + at : total + at + size, length:] = cosine
    upper = jnp.dot(lhs[...], data[...], preferred_element_type=F32).astype(BF16)
    real, imag = upper[:total], upper[total:]
    rhs[:total, :length] = imag
    rhs[:total, length:] = real
    rhs[total:, :length] = -real
    rhs[total:, length:] = imag
    back = jnp.dot(rhs[...], table[...], preferred_element_type=F32)
    for out, place, at, start, size in blocks:
        rows = pl.ds(start, size)
        real, imag = back[at : at + size], back[total + at : total + at + size]
        sens_real, sens_imag = sens[0, rows, :].astype(F32), sens[1, rows, :].astype(F32)
        out[place, 0] = sens_real * real + sens_imag * imag
        out[place, 1] = sens_real * imag - sens_imag * real


def adjoint(groups, me, table, data, sens, ready=None):
    length = sens.shape[1]
    total = sum(size for group in groups for _, size in group)
    return pl.pallas_call(
        partial(adjoint_kernel, groups),
        out_shape=[
            jax.ShapeDtypeStruct((len(group), 2, group[0][1], length), F32) for group in groups
        ],
        in_specs=[SMEM, VMEM, VMEM, VMEM, ANY],
        out_specs=[VMEM] * len(groups),
        scratch_shapes=[pltpu.VMEM((2 * total, 2 * length), BF16)] * 2,
        compiler_params=PARAMS,
        cost_estimate=flops(16 * total * length * length),
        name="adjoint",
    )(me, table, data.reshape(2 * length, length), sens, me if ready is None else ready)


def core_sums(plan, me, table, data, sens):
    terms, ready = {}, None
    for groups in plan:
        results = adjoint([blocks for _, _, blocks in groups], me, table, data, sens, ready)
        terms.update(((name, flip), value) for (name, flip, _), value in zip(groups, results))
        ready = results[0]
    names = [name for name, flip in terms if flip]
    sums = {}
    for name in names:
        theirs = terms[name, 1]
        if sums and isinstance(name, tuple):
            theirs, _ = lax.optimization_barrier((theirs, sums[names[0]]))
        sums[name] = terms[name, 0] + swap_cores(theirs)
    return sums


def columns_kernel(groups, me, table, *refs):
    outs, rows = refs[:-1], refs[-1]
    length = table.shape[1]
    for blocks, out in zip(groups, outs):
        total = sum(size for _, size in blocks)
        at = 0
        for start, size in blocks:
            row = pl.multiple_of(start(me[0]), 16)
            rows[at : at + size, :] = table[pl.ds(pl.multiple_of(length + row, 16), size), :]
            rows[total + at : total + at + size, :] = table[pl.ds(row, size), :]
            at += size
        out[...] = rows[: 2 * total, :].T


def columns(groups, me, table):
    length = table.shape[1]
    totals = [2 * sum(size for _, size in blocks) for blocks in groups]
    return pl.pallas_call(
        partial(columns_kernel, groups),
        out_shape=[jax.ShapeDtypeStruct((length, total), BF16) for total in totals],
        in_specs=[SMEM, VMEM],
        out_specs=[VMEM] * len(groups),
        scratch_shapes=[pltpu.VMEM((max(totals), length), BF16)],
        compiler_params=PARAMS,
        name="columns",
    )(me, table)


def forward_kernel(blocks, stage, me, table, left, sens, *refs):
    pieces, refs = refs[: len(blocks)], refs[len(blocks) :]
    rest, (out, lhs, mid) = refs[:-3], refs[-3:]
    length = sens.shape[1]
    total = sum(size for _, size in blocks)
    at = 0
    for (start, size), piece in zip(blocks, pieces):
        place = pl.ds(pl.multiple_of(start(me[0]), 16), size)
        real, imag = piece[0], piece[1]
        sens_real, sens_imag = sens[0, place, :].astype(F32), sens[1, place, :].astype(F32)
        coil_real = (sens_real * real - sens_imag * imag).astype(BF16)
        coil_imag = (sens_real * imag + sens_imag * real).astype(BF16)
        top, bottom = pl.ds(at, size), pl.ds(total + at, size)
        lhs[top, :length] = -coil_imag
        lhs[top, length:] = coil_real
        lhs[bottom, :length] = coil_real
        lhs[bottom, length:] = coil_imag
        at += size
    middle = jnp.dot(lhs[...], table[...], preferred_element_type=F32).astype(BF16)
    mid[:total, :length] = middle[:total]
    mid[:total, length:] = middle[total:]
    mid[total:, :length] = -middle[total:]
    mid[total:, length:] = middle[:total]
    freq = jnp.dot(left[...], mid[...], preferred_element_type=F32)
    if stage == "first":
        (kspace,) = rest
        out[:, :length] = freq[:, :length] - kspace[0].astype(F32)
        out[:, length:] = freq[:, length:] - kspace[1].astype(F32)
    elif stage == "next":
        (before,) = rest
        out[...] = before[...] + freq
    else:
        before, mask = rest
        weight = mask[...].astype(F32)
        out[0] = (weight * (before[:, :length] + freq[:, :length])).astype(BF16)
        out[1] = (weight * (before[:, length:] + freq[:, length:])).astype(BF16)


def forward(blocks, stage, me, table, left, sens, pieces, rest):
    length = sens.shape[1]
    total = sum(size for _, size in blocks)
    freq = jax.ShapeDtypeStruct((length, 2 * length), F32)
    resid = jax.ShapeDtypeStruct((2, length, length), BF16)
    return pl.pallas_call(
        partial(forward_kernel, blocks, stage),
        out_shape=resid if stage == "last" else freq,
        in_specs=[SMEM] + [VMEM] * (3 + len(pieces) + len(rest)),
        out_specs=VMEM,
        scratch_shapes=[pltpu.VMEM((2 * total, 2 * length), BF16)] * 2,
        compiler_params=PARAMS,
        cost_estimate=flops(16 * total * length * length),
        name="forward",
    )(me, table, left, sens, *pieces, *rest)


def extend_kernel(blocks, me, *refs):
    pieces, (out, to_before, to_after, volume) = refs[:-4], refs[-4:]
    length = volume.shape[1]
    own = out.shape[1] - 16
    for (start, size), piece in zip(blocks, pieces):
        volume[:, pl.ds(pl.multiple_of(start(me[0]), 16), size), :] = piece[...]
    first = me[0] * own
    for at, row, count in (
        (0, (first + length - 8) & (length - 1), 8),
        (8, first, own),
        (8 + own, (first + own) & (length - 1), 8),
    ):
        values = volume[:, pl.ds(pl.multiple_of(row, 8), count), :]
        out[:, at : at + count, :] = values
        if at <= 8:
            to_before[:, at : at + count, :] = values
        if at >= 8:
            to_after[:, at - 8 : at - 8 + count, :] = values


def tv_kernel(own, before, after, kept, arrived, out):
    size = out.shape[1]
    length = out.shape[2]

    def parts(ref, first, count):
        return [ref[part, first : first + count, :] for part in (0, 1)]

    def next_column(values):
        return [pltpu.roll(value, length - 1, 1) for value in values]

    def minus(left, right):
        return [a - b for a, b in zip(left, right)]

    def fluxes(here, slices, rows):
        columns = minus(next_column(here), here)
        squares = TV_SMOOTH
        for change in (slices, rows, columns):
            squares = squares + (change[0] * change[0] + change[1] * change[1])
        weight = lax.rsqrt(squares)
        return [[weight * value for value in change] for change in (slices, rows, columns)]

    count = size + 1
    here = parts(own, 7, count)
    slices, rows, columns = fluxes(
        here, minus(parts(after, 7, count), here), minus(parts(own, 8, count), here)
    )
    back = parts(before, 0, size)
    center = parts(own, 8, size)
    back_slices, _, _ = fluxes(back, minus(center, back), minus(parts(before, 1, size), back))
    for part in (0, 1):
        col = columns[part][1:]
        tv = (
            (back_slices[part] - slices[part][1:])
            + (rows[part][:-1] - rows[part][1:])
            + (pltpu.roll(col, 1, 1) - col)
        )
        gradient = kept[0, part] + arrived[0, part]
        out[part] = center[part] - STEP_SIZE * (gradient + TV_WEIGHT * tv)


def shards(kspace, sensitivity, sampling):
    kspace, sens, sampling = kspace[0, 0], sensitivity[0, 0], sampling[0]
    length = sampling.shape[0]
    count = lax.axis_size("coil")
    slabs = lax.axis_size("slab")
    top = count.bit_length() - 2
    size = length // count
    half = count // 2
    table = jnp.asarray(dft_table(length))
    me = lax.axis_index("coil").astype(jnp.int32).reshape(1)

    mask = sampling.astype(BF16)
    measured = kspace * mask[None]

    orders = bit_orders(count)
    eighth = length // 8
    chunks = CHUNKS if eighth % (16 * half) == 0 or half <= 4 else (4, 4)
    chunks = [rows * eighth for rows in chunks]

    def chunk_block(chunk, flip, place):
        size = chunks[chunk] // half

        def start(device):
            own = [
                sum(((device >> bit) & 1) << step for step, bit in enumerate(order[:-1]))
                for order in orders
            ]
            block = (by_core(device, flip, own) ^ place) * 2 + ((device & 1) ^ flip)
            return sum(chunks[:chunk]) + block * size

        return start, size

    places = halving_order(top - 1)
    middle = len(places) // 2
    sent, kept = [], []
    for chunk in range(len(chunks)):
        blocks = [[chunk_block(chunk, flip, place) for place in places] for flip in (0, 1)]
        sent.append([(("send", chunk), flip, blocks[flip][middle:]) for flip in (0, 1)])
        kept.append([(("keep", chunk), flip, blocks[flip][:middle]) for flip in (0, 1)])
    plan = [
        [sent[0][1]],
        [sent[0][0]] + [own_other[1] for own_other in sent[1:] + kept],
        [own_other[0] for own_other in sent[1:] + kept],
    ]
    sums = core_sums(plan, me, table, measured, sens)
    currents = [(sums["keep", chunk], sums["send", chunk]) for chunk in range(len(chunks))]
    arrived = []
    for current in currents:
        keep, send = current
        current = keep + swap_chips(send, 0)
        for step in range(1, top - 1):
            middle = current.shape[0] // 2
            current = current[:middle] + swap_chips(current[middle:], step)
        current = current[0]
        pieces = {0: current + swap_chips(current, top - 1)}
        for step in reversed(range(top - 1)):
            for place in list(pieces):
                pieces[place | (1 << step)] = swap_chips(pieces[place], step)
        arrived.append(pieces)
    early = [
        (chunk_block(chunk, flip, 0), swap_cores(pieces[0]) if flip else pieces[0])
        for chunk, pieces in enumerate(arrived)
        for flip in (0, 1)
    ]
    late_blocks = [
        [chunk_block(chunk, flip, place) for chunk in range(len(chunks)) for place in range(1, half // 2)]
        for flip in (0, 1)
    ]
    lefts = columns([[b for b, _ in early], *late_blocks], me, table)
    pieces = [p for _, p in early]
    freq = forward([b for b, _ in early], "first", me, table, lefts[0], sens, pieces, [kspace])
    late = [[], []]
    for chunk in arrived:
        for place in range(1, half // 2):
            piece, freq = lax.optimization_barrier((chunk[place], freq))
            late[0].append(piece)
            late[1].append(swap_cores(piece))
    freq = forward(late_blocks[0], "next", me, table, lefts[1], sens, late[0], [freq])
    resid = forward(late_blocks[1], "last", me, table, lefts[2], sens, late[1], [freq, mask])
    late = [*zip(late_blocks[0], late[0]), *zip(late_blocks[1], late[1])]

    parts = [size]

    def row_block(part, flip, place):
        masks = [
            sum(((place >> step) & 1) << bit for step, bit in enumerate(order)) for order in orders
        ]
        first = sum(parts[:part])
        return (
            lambda device: (device ^ flip ^ by_core(device, flip, masks)) * size + first,
            parts[part],
        )

    places = halving_order(top)
    blocks = [[row_block(0, flip, place) for place in places] for flip in (0, 1)]
    middle, quarter = len(places) // 2, len(places) // 4
    passed = [("passed", flip, blocks[flip][middle + quarter :]) for flip in (0, 1)]
    stays = [("stays", flip, blocks[flip][middle : middle + quarter]) for flip in (0, 1)]
    kept = [("keep", flip, blocks[flip][:middle]) for flip in (0, 1)]
    both = [("send", flip, blocks[flip][middle:]) for flip in (0, 1)]
    plan = [[both[1]], [both[0], kept[1]], [kept[0]]]
    sums = core_sums(plan, me, table, resid, sens)
    keep, passed, stays = sums["keep"], sums["send"][quarter:], sums["send"][:quarter]
    for step in range(top - 1):
        middle = keep.shape[0] // 2
        if step:
            passed, stays = send[middle:], send[:middle]
        send = keep[middle:] + swap_chips(passed, step)
        kept = [keep[:middle], swap_chips(stays, step)]
        if step < top - 2:
            keep = kept[0] + kept[1]
    gradient = swap_chips(send, top - 1)

    extended, to_before, to_after = pl.pallas_call(
        partial(extend_kernel, [b for b, _ in early + late]),
        out_shape=[jax.ShapeDtypeStruct((2, size + more, length), F32) for more in (16, 8, 8)],
        in_specs=[SMEM] + [VMEM] * len(early + late),
        out_specs=[VMEM] * 3,
        scratch_shapes=[pltpu.VMEM((2, length, length), F32)],
        compiler_params=PARAMS,
        name="extend",
    )(me, *[p for _, p in early + late])
    ahead = [(i, (i + 1) % slabs) for i in range(slabs)]
    behind = [(target, source) for source, target in ahead]
    before = lax.ppermute(to_after, "slab", ahead)
    after = lax.ppermute(to_before, "slab", behind)
    base = pl.pallas_call(
        tv_kernel,
        out_shape=jax.ShapeDtypeStruct((2, size, length), F32),
        in_specs=[VMEM] * 5,
        out_specs=VMEM,
        compiler_params=PARAMS,
        name="total_variation",
    )(extended, before, after, *kept)
    return (base - STEP_SIZE * gradient[0])[None]


def solution(mesh):
    placed = (
        P("slab", "coil", None, None, None),
        P("slab", "coil", None, None, None),
        P("slab", None, None),
    )
    return jax.shard_map(
        shards, mesh=mesh, in_specs=placed, out_specs=P("slab", None, "coil", None), check_vma=False
    )
```

```python
from functools import partial
import math

import jax
import jax.numpy as jnp
import ml_dtypes
import numpy as np
from jax import lax
from jax.experimental import pallas as pl
from jax.experimental.pallas import tpu as pltpu
from jax.sharding import PartitionSpec as P

STEP_SIZE = 0.25
TV_WEIGHT = 0.5
TV_SMOOTH = 0.25
CHUNKS = (5, 3)

F32 = jnp.float32
BF16 = jnp.bfloat16
VMEM = pl.BlockSpec(memory_space=pltpu.VMEM)
ANY = pl.BlockSpec(memory_space=pl.ANY)
SMEM = pl.BlockSpec(memory_space=pltpu.SMEM)
PARAMS = pltpu.CompilerParams(vmem_limit_bytes=24 * 2**20)


def dft_table(length):
    indices = np.arange(length, dtype=np.int64)
    angles = (indices[:, None] * indices[None, :] % length) * (2.0 * math.pi / length)
    factor = 1.0 / math.sqrt(length)
    table = np.concatenate([-np.sin(angles) * factor, np.cos(angles) * factor])
    return table.astype(ml_dtypes.bfloat16)


def bit_orders(count):
    top = count.bit_length() - 2
    return list(range(1, top + 1)), list(range(top, 0, -1))


def swap_cores(value):
    count = lax.axis_size("coil")
    return lax.ppermute(value, "coil", [(i, i ^ 1) for i in range(count)])


def swap_chips(value, step):
    count = lax.axis_size("coil")
    orders = bit_orders(count)
    return lax.ppermute(
        value, "coil", [(i, i ^ (1 << orders[i & 1][step])) for i in range(count)]
    )


def by_core(device, flip, values):
    return jnp.where((device & 1) ^ flip == 0, values[0], values[1])


def halving_order(steps):
    places = [0]
    for step in reversed(range(steps)):
        places = places + [place | (1 << step) for place in places]
    return places


def flops(cost):
    return pl.CostEstimate(flops=cost, bytes_accessed=4 * 2**20, transcendentals=0)


def adjoint_kernel(groups, me, table, data, sens, ready, *refs):
    del ready
    outs, (lhs, rhs) = refs[: len(groups)], refs[len(groups) :]
    length = sens.shape[1]
    device = me[0]
    blocks, at = [], 0
    for out, group in zip(outs, groups):
        for place, (start, size) in enumerate(group):
            blocks.append((out, place, at, pl.multiple_of(start(device), 16), size))
            at += size
    total = at
    for _, _, at, start, size in blocks:
        sine = table[pl.ds(start, size), :]
        cosine = table[pl.ds(pl.multiple_of(length + start, 16), size), :]
        lhs[at : at + size, :length] = cosine
        lhs[at : at + size, length:] = sine
        lhs[total + at : total + at + size, :length] = -sine
        lhs[total + at : total + at + size, length:] = cosine
    upper = jnp.dot(lhs[...], data[...], preferred_element_type=F32).astype(BF16)
    real, imag = upper[:total], upper[total:]
    rhs[:total, :length] = imag
    rhs[:total, length:] = real
    rhs[total:, :length] = -real
    rhs[total:, length:] = imag
    back = jnp.dot(rhs[...], table[...], preferred_element_type=F32)
    for out, place, at, start, size in blocks:
        rows = pl.ds(start, size)
        real, imag = back[at : at + size], back[total + at : total + at + size]
        sens_real, sens_imag = sens[0, rows, :].astype(F32), sens[1, rows, :].astype(F32)
        out[place, 0] = sens_real * real + sens_imag * imag
        out[place, 1] = sens_real * imag - sens_imag * real


def adjoint(groups, me, table, data, sens, ready=None):
    length = sens.shape[1]
    total = sum(size for group in groups for _, size in group)
    return pl.pallas_call(
        partial(adjoint_kernel, groups),
        out_shape=[
            jax.ShapeDtypeStruct((len(group), 2, group[0][1], length), F32) for group in groups
        ],
        in_specs=[SMEM, VMEM, VMEM, VMEM, ANY],
        out_specs=[VMEM] * len(groups),
        scratch_shapes=[pltpu.VMEM((2 * total, 2 * length), BF16)] * 2,
        compiler_params=PARAMS,
        cost_estimate=flops(16 * total * length * length),
        name="adjoint",
    )(me, table, data.reshape(2 * length, length), sens, me if ready is None else ready)


def core_sums(plan, me, table, data, sens):
    terms, ready = {}, None
    for groups in plan:
        results = adjoint([blocks for _, _, blocks in groups], me, table, data, sens, ready)
        terms.update(((name, flip), value) for (name, flip, _), value in zip(groups, results))
        del results
    names = [name for name, flip in terms if flip]
    sums = {}
    for name in names:
        theirs = terms[name, 1]
        if sums and isinstance(name, tuple):
            theirs, _ = lax.optimization_barrier((theirs, sums[names[0]]))
        sums[name] = terms[name, 0] + swap_cores(theirs)
    return sums


def columns_kernel(groups, me, table, *refs):
    outs, rows = refs[:-1], refs[-1]
    length = table.shape[1]
    for blocks, out in zip(groups, outs):
        total = sum(size for _, size in blocks)
        at = 0
        for start, size in blocks:
            row = pl.multiple_of(start(me[0]), 16)
            rows[at : at + size, :] = table[pl.ds(pl.multiple_of(length + row, 16), size), :]
            rows[total + at : total + at + size, :] = table[pl.ds(row, size), :]
            at += size
        out[...] = rows[: 2 * total, :].T


def columns(groups, me, table):
    length = table.shape[1]
    totals = [2 * sum(size for _, size in blocks) for blocks in groups]
    return pl.pallas_call(
        partial(columns_kernel, groups),
        out_shape=[jax.ShapeDtypeStruct((length, total), BF16) for total in totals],
        in_specs=[SMEM, VMEM],
        out_specs=[VMEM] * len(groups),
        scratch_shapes=[pltpu.VMEM((max(totals), length), BF16)],
        compiler_params=PARAMS,
        name="columns",
    )(me, table)


def forward_kernel(blocks, stage, me, table, left, sens, *refs):
    pieces, refs = refs[: len(blocks)], refs[len(blocks) :]
    rest, (out, lhs, mid) = refs[:-3], refs[-3:]
    length = sens.shape[1]
    total = sum(size for _, size in blocks)
    at = 0
    for (start, size), piece in zip(blocks, pieces):
        place = pl.ds(pl.multiple_of(start(me[0]), 16), size)
        real, imag = piece[0], piece[1]
        sens_real, sens_imag = sens[0, place, :].astype(F32), sens[1, place, :].astype(F32)
        coil_real = (sens_real * real - sens_imag * imag).astype(BF16)
        coil_imag = (sens_real * imag + sens_imag * real).astype(BF16)
        top, bottom = pl.ds(at, size), pl.ds(total + at, size)
        lhs[top, :length] = -coil_imag
        lhs[top, length:] = coil_real
        lhs[bottom, :length] = coil_real
        lhs[bottom, length:] = coil_imag
        at += size
    middle = jnp.dot(lhs[...], table[...], preferred_element_type=F32).astype(BF16)
    mid[:total, :length] = middle[:total]
    mid[:total, length:] = middle[total:]
    mid[total:, :length] = -middle[total:]
    mid[total:, length:] = middle[:total]
    freq = jnp.dot(left[...], mid[...], preferred_element_type=F32)
    if stage == "first":
        (kspace,) = rest
        out[:, :length] = freq[:, :length] - kspace[0].astype(F32)
        out[:, length:] = freq[:, length:] - kspace[1].astype(F32)
    elif stage == "next":
        (before,) = rest
        out[...] = before[...] + freq
    else:
        before, mask = rest
        weight = mask[...].astype(F32)
        out[0] = (weight * (before[:, :length] + freq[:, :length])).astype(BF16)
        out[1] = (weight * (before[:, length:] + freq[:, length:])).astype(BF16)


def forward(blocks, stage, me, table, left, sens, pieces, rest):
    length = sens.shape[1]
    total = sum(size for _, size in blocks)
    freq = jax.ShapeDtypeStruct((length, 2 * length), F32)
    resid = jax.ShapeDtypeStruct((2, length, length), BF16)
    return pl.pallas_call(
        partial(forward_kernel, blocks, stage),
        out_shape=resid if stage == "last" else freq,
        in_specs=[SMEM] + [VMEM] * (3 + len(pieces) + len(rest)),
        out_specs=VMEM,
        scratch_shapes=[pltpu.VMEM((2 * total, 2 * length), BF16)] * 2,
        compiler_params=PARAMS,
        cost_estimate=flops(16 * total * length * length),
        name="forward",
    )(me, table, left, sens, *pieces, *rest)


def extend_kernel(blocks, me, *refs):
    pieces, (out, to_before, to_after, volume) = refs[:-4], refs[-4:]
    length = volume.shape[1]
    own = out.shape[1] - 16
    for (start, size), piece in zip(blocks, pieces):
        volume[:, pl.ds(pl.multiple_of(start(me[0]), 16), size), :] = piece[...]
    first = me[0] * own
    for at, row, count in (
        (0, (first + length - 8) & (length - 1), 8),
        (8, first, own),
        (8 + own, (first + own) & (length - 1), 8),
    ):
        values = volume[:, pl.ds(pl.multiple_of(row, 8), count), :]
        out[:, at : at + count, :] = values
        if at <= 8:
            to_before[:, at : at + count, :] = values
        if at >= 8:
            to_after[:, at - 8 : at - 8 + count, :] = values


def tv_kernel(own, before, after, kept, arrived, out):
    size = out.shape[1]
    length = out.shape[2]

    def parts(ref, first, count):
        return [ref[part, first : first + count, :] for part in (0, 1)]

    def next_column(values):
        return [pltpu.roll(value, length - 1, 1) for value in values]

    def minus(left, right):
        return [a - b for a, b in zip(left, right)]

    def fluxes(here, slices, rows):
        columns = minus(next_column(here), here)
        squares = TV_SMOOTH
        for change in (slices, rows, columns):
            squares = squares + (change[0] * change[0] + change[1] * change[1])
        weight = lax.rsqrt(squares)
        return [[weight * value for value in change] for change in (slices, rows, columns)]

    count = size + 1
    here = parts(own, 7, count)
    slices, rows, columns = fluxes(
        here, minus(parts(after, 7, count), here), minus(parts(own, 8, count), here)
    )
    back = parts(before, 0, size)
    center = parts(own, 8, size)
    back_slices, _, _ = fluxes(back, minus(center, back), minus(parts(before, 1, size), back))
    for part in (0, 1):
        col = columns[part][1:]
        tv = (
            (back_slices[part] - slices[part][1:])
            + (rows[part][:-1] - rows[part][1:])
            + (pltpu.roll(col, 1, 1) - col)
        )
        gradient = kept[0, part] + arrived[0, part]
        out[part] = center[part] - STEP_SIZE * (gradient + TV_WEIGHT * tv)


def shards(kspace, sensitivity, sampling):
    kspace, sens, sampling = kspace[0, 0], sensitivity[0, 0], sampling[0]
    length = sampling.shape[0]
    count = lax.axis_size("coil")
    slabs = lax.axis_size("slab")
    top = count.bit_length() - 2
    size = length // count
    half = count // 2
    table = jnp.asarray(dft_table(length))
    me = lax.axis_index("coil").astype(jnp.int32).reshape(1)

    mask = sampling.astype(BF16)
    measured = kspace * mask[None]

    orders = bit_orders(count)
    eighth = length // 8
    chunks = CHUNKS if eighth % (16 * half) == 0 or half <= 4 else (4, 4)
    chunks = [rows * eighth for rows in chunks]

    def chunk_block(chunk, flip, place):
        size = chunks[chunk] // half

        def start(device):
            own = [
                sum(((device >> bit) & 1) << step for step, bit in enumerate(order[:-1]))
                for order in orders
            ]
            block = (by_core(device, flip, own) ^ place) * 2 + ((device & 1) ^ flip)
            return sum(chunks[:chunk]) + block * size

        return start, size

    places = halving_order(top - 1)
    middle = len(places) // 2
    sent, kept = [], []
    for chunk in range(len(chunks)):
        blocks = [[chunk_block(chunk, flip, place) for place in places] for flip in (0, 1)]
        sent.append([(("send", chunk), flip, blocks[flip][middle:]) for flip in (0, 1)])
        kept.append([(("keep", chunk), flip, blocks[flip][:middle]) for flip in (0, 1)])
    plan = [
        [sent[0][1]],
        [sent[0][0]] + [own_other[1] for own_other in sent[1:] + kept],
        [own_other[0] for own_other in sent[1:] + kept],
    ]
    sums = core_sums(plan, me, table, measured, sens)
    currents = [(sums["keep", chunk], sums["send", chunk]) for chunk in range(len(chunks))]
    arrived = []
    for current in currents:
        keep, send = current
        current = keep + swap_chips(send, 0)
        for step in range(1, top - 1):
            middle = current.shape[0] // 2
            current = current[:middle] + swap_chips(current[middle:], step)
        current = current[0]
        pieces = {0: current + swap_chips(current, top - 1)}
        for step in reversed(range(top - 1)):
            for place in list(pieces):
                pieces[place | (1 << step)] = swap_chips(pieces[place], step)
        arrived.append(pieces)
    early = [
        (chunk_block(chunk, flip, 0), swap_cores(pieces[0]) if flip else pieces[0])
        for chunk, pieces in enumerate(arrived)
        for flip in (0, 1)
    ]
    late_blocks = [
        [chunk_block(chunk, flip, place) for chunk in range(len(chunks)) for place in range(1, half // 2)]
        for flip in (0, 1)
    ]
    lefts = columns([[b for b, _ in early], *late_blocks], me, table)
    pieces = [p for _, p in early]
    freq = forward([b for b, _ in early], "first", me, table, lefts[0], sens, pieces, [kspace])
    late = [[], []]
    for chunk in arrived:
        for place in range(1, half // 2):
            piece, freq = lax.optimization_barrier((chunk[place], freq))
            late[0].append(piece)
            late[1].append(swap_cores(piece))
    freq = forward(late_blocks[0], "next", me, table, lefts[1], sens, late[0], [freq])
    resid = forward(late_blocks[1], "last", me, table, lefts[2], sens, late[1], [freq, mask])
    late = [*zip(late_blocks[0], late[0]), *zip(late_blocks[1], late[1])]

    parts = [size]

    def row_block(part, flip, place):
        masks = [
            sum(((place >> step) & 1) << bit for step, bit in enumerate(order)) for order in orders
        ]
        first = sum(parts[:part])
        return (
            lambda device: (device ^ flip ^ by_core(device, flip, masks)) * size + first,
            parts[part],
        )

    places = halving_order(top)
    blocks = [[row_block(0, flip, place) for place in places] for flip in (0, 1)]
    middle, quarter = len(places) // 2, len(places) // 4
    passed = [("passed", flip, blocks[flip][middle + quarter :]) for flip in (0, 1)]
    stays = [("stays", flip, blocks[flip][middle : middle + quarter]) for flip in (0, 1)]
    kept = [("keep", flip, blocks[flip][:middle]) for flip in (0, 1)]
    both = [("send", flip, blocks[flip][middle:]) for flip in (0, 1)]
    plan = [[both[1]], [both[0], kept[1]], [kept[0]]]
    sums = core_sums(plan, me, table, resid, sens)
    keep, passed, stays = sums["keep"], sums["send"][quarter:], sums["send"][:quarter]
    for step in range(top - 1):
        middle = keep.shape[0] // 2
        if step:
            passed, stays = send[middle:], send[:middle]
        send = keep[middle:] + swap_chips(passed, step)
        kept = [keep[:middle], swap_chips(stays, step)]
        if step < top - 2:
            keep = kept[0] + kept[1]
    gradient = swap_chips(send, top - 1)

    extended, to_before, to_after = pl.pallas_call(
        partial(extend_kernel, [b for b, _ in early + late]),
        out_shape=[jax.ShapeDtypeStruct((2, size + more, length), F32) for more in (16, 8, 8)],
        in_specs=[SMEM] + [VMEM] * len(early + late),
        out_specs=[VMEM] * 3,
        scratch_shapes=[pltpu.VMEM((2, length, length), F32)],
        compiler_params=PARAMS,
        name="extend",
    )(me, *[p for _, p in early + late])
    ahead = [(i, (i + 1) % slabs) for i in range(slabs)]
    behind = [(target, source) for source, target in ahead]
    before = lax.ppermute(to_after, "slab", ahead)
    after = lax.ppermute(to_before, "slab", behind)
    base = pl.pallas_call(
        tv_kernel,
        out_shape=jax.ShapeDtypeStruct((2, size, length), F32),
        in_specs=[VMEM] * 5,
        out_specs=VMEM,
        compiler_params=PARAMS,
        name="total_variation",
    )(extended, before, after, *kept)
    return (base - STEP_SIZE * gradient[0])[None]


def solution(mesh):
    placed = (
        P("slab", "coil", None, None, None),
        P("slab", "coil", None, None, None),
        P("slab", None, None),
    )
    return jax.shard_map(
        shards, mesh=mesh, in_specs=placed, out_specs=P("slab", None, "coil", None), check_vma=False
    )
```
